128 devices in a mesh: gx: 32 (over x_lo, z, y), gy: 4 (over x_hi, core).
Axes of the slice: x: 4 (x_hi: 2, x_lo: 2; x = x_hi * 2 + x_lo), y: 4, z: 4, core: 2. Of those that a mesh axis runs over, the one named last changes fastest.
Arguments:
- field_in: bfloat16 [3, 128, 32, 128], P(None, 'gx', 'gy'), may hold values from -6 to 6
- cotangent: bfloat16 [3, 128, 32, 128], P(None, 'gx', 'gy'), may hold values from -6 to 6
- kernel_one: bfloat16 [64, 3, 3, 3, 3], replicated, may hold values from -0.625 to 0.625
- kernel_two: bfloat16 [27, 4096], replicated, may hold values from -0.15625 to 0.15625
- kernel_three: bfloat16 [27, 4096], replicated, may hold values from -0.15625 to 0.15625
- kernel_four: bfloat16 [3, 64, 3, 3, 3], replicated, may hold values from -0.15625 to 0.15625
Outputs:
- output: float32 [3, 128, 32, 128], P(None, 'gx', 'gy')
- grad_one: float32 [64, 3, 3, 3, 3], replicated
- grad_two: float32 [27, 4096], replicated
- grad_three: float32 [27, 4096], replicated
- grad_four: float32 [3, 64, 3, 3, 3], replicated
The draws below stay inside these ranges and needn't reach their ends.
All inputs are finite; a program needn't handle non-finite values.
Results may differ from the reference program's by a relative error of at most 0.015.
Values may be sent and summed in bfloat16 or wider, within the bound.
No kernel may reach another device: no remote copies, remote signals or barrier semaphores. Data moves between devices by JAX's collectives and lax.ppermute only.
A program may use at most 128 MiB of HBM per device.

```python
import math
import jax
import jax.numpy as jnp
from jax import lax

CIN = 3
C = 64
CZ = 128
NX = 128
NY = 32


def block_scale(own_key, shape, cuts, smallest, largest):
    gain = 1.0
    for axis_at, shards_of in cuts:
        draws = jax.random.uniform(jax.random.fold_in(jax.random.fold_in(own_key, 6), axis_at), (shards_of,), jnp.float32, smallest / len(cuts), largest / len(cuts))
        gain = gain * jnp.repeat(jnp.exp(draws), shape[axis_at] // shards_of).reshape((-1,) + (1,) * (len(shape) - 1 - axis_at))
    return gain


def centred(key, extent, scale, bound, pieces=(), kind=jnp.bfloat16):
    entries = scale * jax.random.normal(key, extent, jnp.float32)
    if pieces:
        entries = entries * block_scale(key, extent, pieces, -0.22, 0.18)
    return jnp.clip(entries, -bound, bound).astype(kind)


def setup_inputs(seed: int = 0) -> dict:
    arg_keys = jax.random.split(jax.random.key(seed), 7)
    return {
        "field_in": centred(arg_keys[0], (CIN, NX, NY, CZ), 1.0, 6.0, ((1, 32), (2, 4))),
        "cotangent": centred(arg_keys[1], (CIN, NX, NY, CZ), 1.0, 6.0, ((1, 32), (2, 4))),
        "kernel_one": centred(arg_keys[2], (C, CIN, 3, 3, 3), (27 * CIN) ** -0.5, 0.625),
        "kernel_two": centred(arg_keys[3], (27, C * C), (27 * C) ** -0.5, 0.15625),
        "kernel_three": centred(arg_keys[4], (27, C * C), (27 * C) ** -0.5, 0.15625),
        "kernel_four": centred(arg_keys[5], (CIN, C, 3, 3, 3), (27 * C) ** -0.5, 0.15625),
    }


NUMBERS = ('NCDHW', 'OIDHW', 'NCDHW')

def conv_valid(padded, kernel):
    return lax.conv_general_dilated(padded[None], kernel, (1, 1, 1), 'VALID', dimension_numbers=NUMBERS, preferred_element_type=jnp.float32)[0]

def weight_grad(padded, gradient):
    result = lax.conv_general_dilated(padded[:, None], gradient[:, None], (1, 1, 1), 'VALID', dimension_numbers=NUMBERS, preferred_element_type=jnp.float32)
    return jnp.transpose(result, (1, 0, 2, 3, 4))

def unpack(kernel):
    width = int(math.isqrt(kernel.shape[1]))
    return jnp.transpose(kernel.reshape(3, 3, 3, width, width), (3, 4, 0, 1, 2))

def packed(grad):
    return jnp.transpose(grad, (2, 3, 4, 0, 1)).reshape(27, grad.shape[0] * grad.shape[1])

def flipped(kernel):
    return jnp.transpose(jnp.flip(kernel, (2, 3, 4)), (1, 0, 2, 3, 4))

def wrap_pad(values):
    return jnp.pad(values, ((0, 0), (1, 1), (1, 1), (1, 1)), mode='wrap')

def leaky(values):
    return 0.1 * values + 0.9 * values * jax.nn.sigmoid(values)

def slope(values):
    sigma = jax.nn.sigmoid(values)
    return 0.1 + 0.9 * sigma * (1.0 + values * (1.0 - sigma))

def block_sum(values):
    shape = values.shape
    blocks = values.astype(jnp.float32).reshape(shape[0], shape[1] // 2, 2, shape[2] // 2, 2, shape[3] // 2, 2)
    return lax.optimization_barrier(jnp.sum(blocks, axis=(2, 4, 6)))

def spread(values):
    return jnp.repeat(jnp.repeat(jnp.repeat(values, 2, axis=1), 2, axis=2), 2, axis=3)

def reference(field_in, cotangent, kernel_one, kernel_two, kernel_three, kernel_four):
    inner_two = unpack(kernel_two)
    inner_three = unpack(kernel_three)
    padded_in = wrap_pad(field_in)
    first_pre = conv_valid(padded_in, kernel_one)
    first_act = leaky(first_pre).astype(jnp.bfloat16)
    padded_first = wrap_pad(first_act)
    second_pre = conv_valid(padded_first, inner_two)
    second_act = leaky(second_pre).astype(jnp.bfloat16)
    coarse_in = (block_sum(second_act) * 0.125).astype(jnp.bfloat16)
    padded_coarse = wrap_pad(coarse_in)
    coarse_pre = conv_valid(padded_coarse, inner_three)
    coarse_act = leaky(coarse_pre).astype(jnp.bfloat16)
    skip_sum = (second_act.astype(jnp.float32) + spread(coarse_act.astype(jnp.float32))).astype(jnp.bfloat16)
    padded_skip = wrap_pad(skip_sum)
    output = conv_valid(padded_skip, kernel_four) + field_in.astype(jnp.float32)
    scale = 1.0 / math.sqrt(NX * NY * CZ)
    out_grad = (cotangent.astype(jnp.float32) * scale).astype(jnp.bfloat16)
    grad_four = weight_grad(padded_skip, out_grad)
    skip_grad = conv_valid(wrap_pad(out_grad), flipped(kernel_four))
    coarse_grad = (block_sum(skip_grad) * slope(coarse_pre)).astype(jnp.bfloat16)
    grad_three = packed(weight_grad(padded_coarse, coarse_grad))
    pooled_grad = conv_valid(wrap_pad(coarse_grad), flipped(inner_three))
    second_grad = ((skip_grad + spread(pooled_grad) * 0.125) * slope(second_pre)).astype(jnp.bfloat16)
    grad_two = packed(weight_grad(padded_first, second_grad))
    first_back = conv_valid(wrap_pad(second_grad), flipped(inner_two))
    first_grad = (first_back * slope(first_pre)).astype(jnp.bfloat16)
    grad_one = weight_grad(padded_in, first_grad)
    return (output, grad_one, grad_two, grad_three, grad_four)
```

```python
import math

import jax
import jax.numpy as jnp
from jax import lax
from jax.experimental import pallas as pl
from jax.experimental.pallas import tpu as pltpu
from jax.sharding import PartitionSpec as P

F32 = jnp.float32
BF16 = jnp.bfloat16
AXES = ("gx", "gy")
HALO = 8
CH = 64
LANES = 128


def shifted(block, axis, steps):
    count = lax.axis_size(axis)
    return lax.ppermute(block, axis, [(i, (i + steps) % count) for i in range(count)])


def toeplitz_rows(taps):
    low = jnp.pad(taps, ((0, 0), (0, 1), (0, 0), (0, 0), (0, 0)))
    high = jnp.pad(taps, ((0, 0), (1, 0), (0, 0), (0, 0), (0, 0)))
    both = jnp.stack([low, high])
    both = jnp.transpose(both, (0, 3, 4, 1, 2, 5))
    return both.reshape(6 * taps.shape[3], 12 * taps.shape[4])


def toeplitz_window(taps):
    out = taps.shape[0]
    taps = jnp.pad(taps, ((0, 0), (0, 0), (0, 0), (0, 1), (0, 1))).reshape(out, 3, 3, 16)
    rows = [
        jnp.pad(taps, ((0, 0), (dx, 1 - dx), (dy, 1 - dy), (0, 0)))
        for dx in range(2)
        for dy in range(2)
    ]
    return jnp.stack(rows).reshape(4 * out, 256)


def swapped(taps):
    return jnp.swapaxes(jnp.flip(taps, (0, 1, 2)), 3, 4)


def leaky(values):
    return values * (0.55 + 0.45 * jnp.tanh(0.5 * values))


def slope(values):
    sigma = 0.5 + 0.5 * jnp.tanh(0.5 * values)
    return 0.1 + 0.9 * sigma * (1.0 + values * (1.0 - sigma))


def turned(values, steps):
    return pltpu.roll(values, steps % LANES, values.ndim - 1)


def four_columns(source, weights, x, y, step):
    rows = [source[x + r, pl.ds(y, 4)].reshape(4 * CH, LANES) for r in range(4)]
    window = jnp.concatenate(
        [jnp.concatenate([rows[a], rows[a + 1]], axis=1) for a in range(3)], axis=0
    )
    product = jnp.dot(weights[...], window, preferred_element_type=F32)
    out = product.shape[0] // 6
    result = []
    for dx in range(2):
        line = []
        for dy in range(2):
            part = product[3 * out * dy : 3 * out * (dy + 1), LANES * dx : LANES * (dx + 1)]
            line.append(
                turned(part[:out], step) + part[out : 2 * out] + turned(part[2 * out :], -step)
            )
        result.append(line)
    return result


def window_row(source, weights, x, y, blocks):
    parts = []
    for k in range(blocks):
        rows = [source[x + r, pl.ds(y + 2 * k, 4)].reshape(64, LANES) for r in range(4)]
        parts.append(jnp.concatenate(rows, axis=0))
    return jnp.dot(weights[...], jnp.concatenate(parts, axis=1), preferred_element_type=F32)


def line(source, x, y, count):
    return jnp.concatenate([source[x, y + k] for k in range(count)], axis=1)


def neighbour_lines(source, x, y, count):
    return [line(source, x + a - 1, y + b - 1, count) for a in range(3) for b in range(3)]


def contract(left, right):
    return lax.dot_general(left, right, (((1,), (1,)), ((), ())), preferred_element_type=F32)


def pair_sum(values):
    lane = lax.broadcasted_iota(jnp.int32, values.shape, 1)
    return values + jnp.where(lane % 2 == 0, turned(values, -1), turned(values, 1))


def step_kernel(
    scale,
    nx,
    ny,
    g_ref,
    t1_ref,
    t2_ref,
    t2b_ref,
    t3_ref,
    t3b_ref,
    t4_ref,
    t4b_ref,
    out_ref,
    grads_ref,
    f1,
    f2,
    a1,
    p1,
    a2,
    p2,
    sg,
    ci,
    ca,
    cg,
    pg,
    sk,
    g2,
    g3,
    c3,
    g1,
    acc2,
    acc3,
    acc4,
    acc1,
):
    wide, tall = nx + 2 * HALO, ny + 2 * HALO

    @pl.loop(0, wide)
    def _(x):
        cells = g_ref[x].astype(F32)
        low = lax.broadcasted_iota(jnp.int32, cells.shape, 1) < 4

        def rows(values, first):
            before, after = turned(values, 1), turned(values, -1)
            zero = jnp.zeros_like(values)
            if first:
                top = jnp.where(low, before, pltpu.roll(values, 4, 1))
                bottom = jnp.where(low, after, zero)
            else:
                top = jnp.where(low, pltpu.roll(before, 4, 1), values)
                bottom = jnp.where(low, pltpu.roll(after, 4, 1), zero)
            return jnp.concatenate([top, bottom], axis=1).astype(BF16)

        f1[x] = rows(cells, True)
        f2[x] = rows(cells * scale, False)

    @pl.loop(0, (nx + 8) // 2)
    def _(i):
        blocks = (ny + 8) // 2
        product = window_row(f2, t4b_ref, 2 * i + 3, 3, blocks)
        for k in range(blocks):
            for dx in range(2):
                for dy in range(2):
                    at = (2 * dx + dy) * CH
                    sg[2 * i + dx, 2 * k + dy] = product[
                        at : at + CH, LANES * k : LANES * (k + 1)
                    ]

    @pl.loop(0, (nx + 14) // 2)
    def _(i):
        blocks = (ny + 14) // 2
        product = window_row(f1, t1_ref, 2 * i, 0, blocks)
        for k in range(blocks):
            for dx in range(2):
                for dy in range(2):
                    at = (2 * dx + dy) * CH
                    value = product[at : at + CH, LANES * k : LANES * (k + 1)]
                    a1[2 * i + dx, 2 * k + dy] = leaky(value).astype(BF16)
                    y = 2 * k + dy - 7
                    if 0 <= y < ny:
                        p1[2 * i + dx, y] = value

    @pl.loop(0, (nx + 12) // 2)
    def _(i):
        @pl.loop(0, (ny + 12) // 4)
        def _(j2):
            for half in range(2):
                j = 2 * j2 + half
                values = four_columns(a1, t2_ref, 2 * i, 2 * j, 1)
                total = None
                for dx in range(2):
                    for dy in range(2):
                        act = leaky(values[dx][dy]).astype(BF16)
                        p2[2 * i + dx, 2 * j + dy] = values[dx][dy]
                        a2[2 * i + dx, 2 * j + dy] = act
                        act = act.astype(F32)
                        total = act if total is None else total + act
                ci[i, j] = (pair_sum(total) * 0.125).astype(BF16)

    cx, cy = nx // 2, ny // 2

    @pl.loop(0, (cx + 4) // 2)
    def _(i):
        @pl.loop(0, (cy + 4) // 2)
        def _(j):
            values = four_columns(ci, t3_ref, 2 * i, 2 * j, 2)
            for dx in range(2):
                for dy in range(2):
                    x, y = 2 * i + dx, 2 * j + dy
                    ca[x, y] = leaky(values[dx][dy]).astype(BF16)
                    total = (
                        sg[2 * x, 2 * y]
                        + sg[2 * x, 2 * y + 1]
                        + sg[2 * x + 1, 2 * y]
                        + sg[2 * x + 1, 2 * y + 1]
                    )
                    cg[x, y] = (pair_sum(total) * slope(values[dx][dy])).astype(BF16)

    @pl.loop(0, (cx + 2) // 2)
    def _(i):
        @pl.loop(0, (cy + 2) // 2)
        def _(j):
            values = four_columns(cg, t3b_ref, 2 * i, 2 * j, 2)
            for dx in range(2):
                for dy in range(2):
                    pg[2 * i + dx, 2 * j + dy] = values[dx][dy]

    @pl.loop(0, nx + 2)
    def _(x):
        up = (x + 1) // 2
        for y in range(ny + 2):
            right = (y + 1) // 2
            sk[x, y] = (
                a2[x + 5, y + 5].astype(F32) + ca[up + 1, right + 1].astype(F32)
            ).astype(BF16)
            g2[x, y] = (
                (sg[x + 3, y + 3] + pg[up, right] * 0.125) * slope(p2[x + 5, y + 5])
            ).astype(BF16)

    @pl.loop(0, nx)
    def _(x):
        for y in range(ny):
            middle = g2[x + 1, y + 1]
            value = middle.astype(F32)
            g3[x, y] = jnp.concatenate(
                [turned(value, -1).astype(BF16), middle, turned(value, 1).astype(BF16)], axis=0
            )

    for x in range(cx):
        for y in range(cy):
            middle = cg[x + 2, y + 2]
            value = middle.astype(F32)
            c3[x, y] = jnp.concatenate(
                [turned(value, -2).astype(BF16), middle, turned(value, 2).astype(BF16)], axis=0
            )

    @pl.loop(0, nx // 2)
    def _(i):
        @pl.loop(0, ny // 2)
        def _(j):
            values = four_columns(sk, t4_ref, 2 * i, 2 * j, 1)
            for dx in range(2):
                for dy in range(2):
                    x, y = 2 * i + dx, 2 * j + dy
                    out_ref[x, y] = values[dx][dy] + g_ref[x + HALO, y + HALO].astype(F32)

    @pl.loop(0, nx // 2)
    def _(i):
        @pl.loop(0, ny // 2)
        def _(j):
            values = four_columns(g2, t2b_ref, 2 * i, 2 * j, 1)
            for dx in range(2):
                for dy in range(2):
                    x, y = 2 * i + dx, 2 * j + dy
                    g1[x, y] = (values[dx][dy] * slope(p1[x + 7, y])).astype(BF16)

    acc2[...] = jnp.zeros_like(acc2)
    acc3[...] = jnp.zeros_like(acc3)
    acc4[...] = jnp.zeros_like(acc4)
    acc1[...] = jnp.zeros_like(acc1)
    blank = jnp.zeros((CH, ny * LANES), BF16)

    @pl.loop(0, nx)
    def _(x):
        acc2[...] += contract(
            line(g3, x, 0, ny),
            jnp.concatenate(neighbour_lines(a1, x + 7, 7, ny) + [blank], axis=0),
        )
        acc4[...] += contract(
            line(f2, x + HALO, HALO, ny),
            jnp.concatenate(neighbour_lines(sk, x + 1, 1, ny) + [blank], axis=0),
        )
        acc1[...] += contract(
            jnp.concatenate(neighbour_lines(f1, x + HALO, HALO, ny), axis=0),
            jnp.concatenate([line(g1, x, 0, ny), blank], axis=0),
        )

    blank = jnp.zeros((CH, cy * LANES), BF16)
    for x in range(cx):
        acc3[...] += contract(
            line(c3, x, 0, cy),
            jnp.concatenate(neighbour_lines(ci, x + 3, 3, cy) + [blank], axis=0),
        )

    acc3[...] = acc3[...] * 0.5
    for k in range(4):
        grads_ref[192 * k : 192 * (k + 1)] = acc2[:, LANES * k : LANES * (k + 1)].astype(BF16)
        grads_ref[768 + 192 * k : 960 + 192 * k] = acc3[:, LANES * k : LANES * (k + 1)].astype(
            BF16
        )
    grads_ref[1536:1728] = (acc2[:, 512:] + turned(acc3[:, 512:], 64)).astype(BF16)
    for k in range(5):
        grads_ref[1728 + 16 * k : 1744 + 16 * k] = acc4[:, LANES * k : LANES * (k + 1)].astype(
            BF16
        )
    grads_ref[1808:1952] = acc1[...].astype(BF16)
    grads_ref[1952:] = jnp.zeros((96, LANES), BF16)


def body(field_in, cotangent, kernel_one, kernel_two, kernel_three, kernel_four):
    nx, ny, nz = field_in.shape[1:]
    devices = lax.axis_size("gx") * lax.axis_size("gy")
    scale = 1.0 / math.sqrt(nx * ny * nz * devices)

    blank = jnp.zeros((1, nx, ny, nz), BF16)
    block = jnp.concatenate([field_in, blank, cotangent, blank], axis=0)
    block = jnp.transpose(block, (1, 2, 0, 3))
    block = jnp.concatenate(
        [
            shifted(block, "gx", 2),
            shifted(block, "gx", 1),
            block,
            shifted(block, "gx", -1),
            shifted(block, "gx", -2),
        ],
        axis=0,
    )
    block = jnp.concatenate(
        [shifted(block, "gy", 1), block, shifted(block, "gy", -1)], axis=1
    )

    two = kernel_two.reshape(3, 3, 3, CH, CH)
    three = kernel_three.reshape(3, 3, 3, CH, CH)
    four = jnp.transpose(kernel_four, (2, 3, 4, 0, 1))
    weights = (
        toeplitz_window(jnp.transpose(kernel_one, (0, 2, 3, 4, 1))),
        toeplitz_rows(two),
        toeplitz_rows(swapped(two)),
        toeplitz_rows(three),
        toeplitz_rows(swapped(three)),
        toeplitz_rows(jnp.pad(four, ((0, 0), (0, 0), (0, 0), (0, 5), (0, 0)))),
        toeplitz_window(jnp.transpose(swapped(four), (3, 0, 1, 2, 4))),
    )

    wide, tall = nx + 2 * HALO, ny + 2 * HALO
    cx, cy = nx // 2, ny // 2

    def fine(more, kind, rows=CH):
        return pltpu.VMEM((nx + 2 * more, ny + 2 * more, rows, LANES), kind)

    def coarse(more, kind, rows=CH):
        return pltpu.VMEM((cx + 2 * more, cy + 2 * more, rows, LANES), kind)

    out, grads = pl.pallas_call(
        lambda *refs: step_kernel(scale, nx, ny, *refs),
        out_shape=(
            jax.ShapeDtypeStruct((nx, ny, 8, LANES), F32),
            jax.ShapeDtypeStruct((2048, LANES), BF16),
        ),
        in_specs=[pl.BlockSpec(memory_space=pltpu.VMEM)] * 8,
        out_specs=(pl.BlockSpec(memory_space=pltpu.VMEM),) * 2,
        scratch_shapes=[
            fine(HALO, BF16, 16),
            fine(HALO, BF16, 16),
            fine(7, BF16),
            pltpu.VMEM((nx + 14, ny, CH, LANES), F32),
            fine(6, BF16),
            fine(6, F32),
            fine(4, F32),
            coarse(3, BF16),
            coarse(2, BF16),
            coarse(2, BF16),
            coarse(1, F32),
            fine(1, BF16),
            fine(1, BF16),
            fine(0, BF16, 3 * CH),
            coarse(0, BF16, 3 * CH),
            fine(0, BF16),
            pltpu.VMEM((3 * CH, 640), F32),
            pltpu.VMEM((3 * CH, 640), F32),
            pltpu.VMEM((16, 640), F32),
            pltpu.VMEM((144, LANES), F32),
        ],
        compiler_params=pltpu.CompilerParams(vmem_limit_bytes=60 * 1024 * 1024),
    )(block, *weights)

    output = jnp.transpose(out[:, :, :3], (2, 0, 1, 3))

    share = lax.all_to_all(grads.reshape(devices, -1, LANES), AXES, 0, 0, tiled=True)
    total = jnp.sum(share.astype(F32), axis=0).astype(BF16)
    total = jnp.broadcast_to(total[None], (devices,) + total.shape)
    total = lax.all_to_all(total, AXES, 0, 0, tiled=True).reshape(2048, LANES)

    def inner(first, rest):
        lanes = [total[first + 192 * k : first + 192 * (k + 1)] for k in range(4)]
        full = jnp.concatenate(lanes + [rest], axis=1).reshape(3, CH, 9, CH)
        return jnp.transpose(full, (2, 0, 1, 3)).reshape(27, CH * CH).astype(F32)

    grad_two = inner(0, total[1536:1728, :CH])
    grad_three = inner(768, total[1536:1728, CH:])
    last = jnp.concatenate(
        [total[1728 + 16 * k : 1744 + 16 * k] for k in range(5)], axis=1
    )[:12, : 9 * CH].reshape(3, 4, 3, 3, CH)[::-1, :3]
    grad_four = jnp.transpose(last, (1, 4, 2, 3, 0)).astype(F32)
    first = total[1808:1952, :CH].reshape(3, 3, 4, 4, CH)[:, :, :3, :3]
    grad_one = jnp.transpose(first, (4, 3, 0, 1, 2)).astype(F32)
    return (output, grad_one, grad_two, grad_three, grad_four)


def solution(mesh):
    return jax.shard_map(
        body,
        mesh=mesh,
        in_specs=(P(None, "gx", "gy", None), P(None, "gx", "gy", None), P(), P(), P(), P()),
        out_specs=(P(None, "gx", "gy", None), P(), P(), P(), P()),
        check_vma=False,
    )
```

```python
import math

import jax
import jax.numpy as jnp
from jax import lax
from jax.experimental import pallas as pl
from jax.experimental.pallas import tpu as pltpu
from jax.sharding import PartitionSpec as P

F32 = jnp.float32
BF16 = jnp.bfloat16
AXES = ("gx", "gy")
HALO = 8
CH = 64
LANES = 128


def shifted(block, axis, steps):
    count = lax.axis_size(axis)
    return lax.ppermute(block, axis, [(i, (i + steps) % count) for i in range(count)])


def toeplitz_rows(taps):
    low = jnp.pad(taps, ((0, 0), (0, 1), (0, 0), (0, 0), (0, 0)))
    high = jnp.pad(taps, ((0, 0), (1, 0), (0, 0), (0, 0), (0, 0)))
    both = jnp.stack([low, high])
    both = jnp.transpose(both, (0, 3, 4, 1, 2, 5))
    return both.reshape(6 * taps.shape[3], 12 * taps.shape[4])


def weights_kernel(two_ref, three_ref, t2_ref, t2b_ref, t3_ref, t3b_ref):
    row, column = (lax.broadcasted_iota(jnp.int32, (CH, CH), axis) for axis in range(2))
    eye = (row == column).astype(BF16)
    zero = jnp.zeros((CH, CH), BF16)
    for source, forward, backward in (
        (two_ref, t2_ref, t2b_ref),
        (three_ref, t3_ref, t3b_ref),
    ):
        for a in range(3):
            for e in range(3):
                taps = [source[9 * a + 3 * b + e] for b in range(3)]
                plain = jnp.concatenate([tap.astype(F32) for tap in taps + [zero]], axis=1)
                turn = contract(eye, jnp.concatenate(taps[::-1] + [zero], axis=0))
                for target, values, at, lane in (
                    (forward, plain, CH * e, 4 * CH * a),
                    (backward, turn, CH * (2 - e), 4 * CH * (2 - a)),
                ):
                    lanes = slice(lane, lane + 4 * CH)
                    target[at : at + CH, lanes] = values.astype(BF16)
                    moved = pltpu.roll(values, CH, 1).astype(BF16)
                    target[at + 3 * CH : at + 4 * CH, lanes] = moved


def toeplitz_window(taps):
    out = taps.shape[0]
    taps = jnp.pad(taps, ((0, 0), (0, 0), (0, 0), (0, 1), (0, 1))).reshape(out, 3, 3, 16)
    rows = [
        jnp.pad(taps, ((0, 0), (dx, 1 - dx), (dy, 1 - dy), (0, 0)))
        for dx in range(2)
        for dy in range(2)
    ]
    return jnp.stack(rows).reshape(4 * out, 256)


def swapped(taps):
    return jnp.swapaxes(jnp.flip(taps, (0, 1, 2)), 3, 4)


def leaky(values):
    return values * (0.55 + 0.45 * jnp.tanh(0.5 * values))


def slope(values):
    sigma = 0.5 + 0.5 * jnp.tanh(0.5 * values)
    return 0.1 + 0.9 * sigma * (1.0 + values * (1.0 - sigma))


def turned(values, steps):
    return pltpu.roll(values, steps % LANES, values.ndim - 1)


def window_of(source, x, y):
    rows = [source[x + r, pl.ds(y, 4)].reshape(4 * CH, LANES) for r in range(4)]
    return jnp.concatenate(
        [jnp.concatenate([rows[a], rows[a + 1]], axis=1) for a in range(3)], axis=0
    )


def product_pair(source, weights, x, y):
    window = jnp.concatenate([window_of(source, x, y), window_of(source, x, y + 2)], axis=1)
    return jnp.dot(weights[...], window, preferred_element_type=F32)


def column_of(product, dx, dy, step):
    out = product.shape[0] // 6
    rows, lane = 3 * out * (dy % 2), LANES * (dx + 2 * (dy // 2))
    first, second, third = (
        product[rows + out * e : rows + out * (e + 1), lane : lane + LANES] for e in range(3)
    )
    return turned(first, step) + second + turned(third, -step)


def pipelined(count, product, finish, even, odd):
    odd[...] = jnp.zeros_like(odd)

    @pl.loop(0, count // 2)
    def _(u):
        even[...] = product(2 * u)
        finish(jnp.maximum(2 * u - 1, 0), odd)
        odd[...] = product(2 * u + 1)
        finish(2 * u, even)

    if count % 2:
        even[...] = product(count - 1)
        finish(count - 2, odd)
        finish(count - 1, even)
    else:
        finish(count - 1, odd)


def window_row(source, weights, x, y, blocks):
    parts = []
    for k in range(blocks):
        rows = [source[x + r, pl.ds(y + 2 * k, 4)].reshape(64, LANES) for r in range(4)]
        parts.append(jnp.concatenate(rows, axis=0))
    return jnp.dot(weights[...], jnp.concatenate(parts, axis=1), preferred_element_type=F32)


def line(source, x, y, count):
    return jnp.concatenate([source[x, y + k] for k in range(count)], axis=1)


def neighbour_lines(source, x, y, count):
    return [line(source, x + a - 1, y + b - 1, count) for a in range(3) for b in range(3)]


def contract(left, right):
    return lax.dot_general(left, right, (((1,), (1,)), ((), ())), preferred_element_type=F32)


def three_taps(value, step):
    return jnp.concatenate([turned(value, -step), value, turned(value, step)], axis=0).astype(BF16)


def tap_rows(total, tap):
    place, e = tap // 3, tap % 3
    tile = slice(LANES * (place // 2), LANES * (place // 2 + 1))
    even = total[CH * e : CH * e + 32, tile]
    odd = total[CH * e + 32 : CH * (e + 1), tile]
    left = lax.broadcasted_iota(jnp.int32, even.shape, 1) < CH
    if place % 2 == 0:
        return jnp.where(left, even, turned(odd, CH))
    return jnp.where(left, turned(even, CH), odd)


def pair_sum(values):
    lane = lax.broadcasted_iota(jnp.int32, values.shape, 1)
    return values + jnp.where(lane % 2 == 0, turned(values, -1), turned(values, 1))


def step_kernel(
    scale,
    nx,
    ny,
    g_ref,
    t1_ref,
    t2_ref,
    t2b_ref,
    t3_ref,
    t3b_ref,
    t4_ref,
    t4b_ref,
    out_ref,
    grads_ref,
    f1,
    f2,
    a1,
    p1,
    a2,
    p2,
    sg,
    ci,
    ca,
    cg,
    pg,
    sk,
    g2,
    g3,
    c3,
    g1,
    acc2,
    acc3,
    acc4,
    acc1,
    even,
    odd,
):
    wide, tall = nx + 2 * HALO, ny + 2 * HALO

    @pl.loop(0, wide)
    def _(x):
        cells = g_ref[x].astype(F32)
        low = lax.broadcasted_iota(jnp.int32, cells.shape, 1) < 4

        def rows(values, first):
            before, after = turned(values, 1), turned(values, -1)
            zero = jnp.zeros_like(values)
            if first:
                top = jnp.where(low, before, pltpu.roll(values, 4, 1))
                bottom = jnp.where(low, after, zero)
            else:
                top = jnp.where(low, pltpu.roll(before, 4, 1), values)
                bottom = jnp.where(low, pltpu.roll(after, 4, 1), zero)
            return jnp.concatenate([top, bottom], axis=1).astype(BF16)

        f1[x] = rows(cells, True)
        f2[x] = rows(cells * scale, False)

    @pl.loop(0, (nx + 8) // 2)
    def _(i):
        blocks = (ny + 8) // 2
        product = window_row(f2, t4b_ref, 2 * i + 3, 3, blocks)
        for k in range(blocks):
            for dx in range(2):
                for dy in range(2):
                    at = (2 * dx + dy) * CH
                    sg[2 * i + dx, 2 * k + dy] = product[
                        at : at + CH, LANES * k : LANES * (k + 1)
                    ]

    @pl.loop(0, (nx + 14) // 2)
    def _(i):
        blocks = (ny + 14) // 2
        product = window_row(f1, t1_ref, 2 * i, 0, blocks)
        for k in range(blocks):
            for dx in range(2):
                for dy in range(2):
                    at = (2 * dx + dy) * CH
                    value = product[at : at + CH, LANES * k : LANES * (k + 1)]
                    a1[2 * i + dx, 2 * k + dy] = leaky(value).astype(BF16)
                    y = 2 * k + dy - 7
                    if 0 <= y < ny:
                        p1[2 * i + dx, y] = value

    pairs = (ny + 12) // 4

    def second_product(t):
        return product_pair(a1, t2_ref, 2 * (t // pairs), 4 * (t % pairs))

    def second_finish(t, product):
        i, j = t // pairs, t % pairs
        for half in range(2):
            total = None
            for dx in range(2):
                for dy in range(2):
                    value = column_of(product, dx, 2 * half + dy, 1)
                    x, y = 2 * i + dx, 4 * j + 2 * half + dy
                    act = leaky(value).astype(BF16)
                    p2[x, y] = value
                    a2[x, y] = act
                    act = act.astype(F32)
                    total = act if total is None else total + act
            ci[i, 2 * j + half] = (pair_sum(total) * 0.125).astype(BF16)

    pipelined((nx + 12) // 2 * pairs, second_product, second_finish, even, odd)

    cx, cy = nx // 2, ny // 2
    coarse_pairs = (cy + 4) // 4

    def coarse_product(t):
        return product_pair(ci, t3_ref, 2 * (t // coarse_pairs), 4 * (t % coarse_pairs))

    def coarse_finish(t, product):
        for dx in range(2):
            for dy in range(4):
                value = column_of(product, dx, dy, 2)
                x, y = 2 * (t // coarse_pairs) + dx, 4 * (t % coarse_pairs) + dy
                ca[x, y] = leaky(value).astype(BF16)
                total = (
                    sg[2 * x, 2 * y]
                    + sg[2 * x, 2 * y + 1]
                    + sg[2 * x + 1, 2 * y]
                    + sg[2 * x + 1, 2 * y + 1]
                )
                cg[x, y] = (pair_sum(total) * slope(value)).astype(BF16)

    pipelined((cx + 4) // 2 * coarse_pairs, coarse_product, coarse_finish, even, odd)

    @pl.loop(0, (cx + 2) // 2)
    def _(i):
        blocks = (cy + 2) // 2
        window = jnp.concatenate([window_of(cg, 2 * i, 2 * j) for j in range(blocks)], axis=1)
        product = jnp.dot(t3b_ref[...], window, preferred_element_type=F32)
        for dx in range(2):
            for dy in range(2 * blocks):
                pg[2 * i + dx, dy] = column_of(product, dx, dy, 2)

    @pl.loop(0, nx + 2)
    def _(x):
        up = (x + 1) // 2
        for y in range(ny + 2):
            right = (y + 1) // 2
            sk[x, y] = (
                a2[x + 5, y + 5].astype(F32) + ca[up + 1, right + 1].astype(F32)
            ).astype(BF16)
            g2[x, y] = (
                (sg[x + 3, y + 3] + pg[up, right] * 0.125) * slope(p2[x + 5, y + 5])
            ).astype(BF16)

    row, column = (lax.broadcasted_iota(jnp.int32, (CH, CH), axis) for axis in range(2))
    parity = (column == 2 * (row % 32) + row // 32).astype(BF16)

    @pl.loop(0, nx)
    def _(x):
        values = jnp.dot(parity, line(g2, x + 1, 1, ny), preferred_element_type=F32)
        for y in range(ny):
            value = values[:, LANES * y : LANES * (y + 1)]
            g3[x, y] = three_taps(value, 1)

    for x in range(cx):
        values = jnp.dot(parity, line(cg, x + 2, 2, cy), preferred_element_type=F32)
        for y in range(cy):
            c3[x, y] = three_taps(values[:, LANES * y : LANES * (y + 1)], 2)

    @pl.loop(0, nx // 2)
    def _(i):
        blocks = ny // 2
        window = jnp.concatenate([window_of(sk, 2 * i, 2 * j) for j in range(blocks)], axis=1)
        product = jnp.dot(t4_ref[...], window, preferred_element_type=F32)
        for dx in range(2):
            for dy in range(ny):
                x = 2 * i + dx
                out_ref[x, dy] = column_of(product, dx, dy, 1) + g_ref[
                    x + HALO, dy + HALO
                ].astype(F32)

    fine_pairs = ny // 4

    def back_product(t):
        return product_pair(g2, t2b_ref, 2 * (t // fine_pairs), 4 * (t % fine_pairs))

    def back_finish(t, product):
        for dx in range(2):
            for dy in range(4):
                x, y = 2 * (t // fine_pairs) + dx, 4 * (t % fine_pairs) + dy
                value = column_of(product, dx, dy, 1)
                g1[x, y] = (value * slope(p1[x + 7, y])).astype(BF16)

    pipelined(nx // 2 * fine_pairs, back_product, back_finish, even, odd)

    acc2[...] = jnp.zeros_like(acc2)
    acc3[...] = jnp.zeros_like(acc3)
    acc4[...] = jnp.zeros_like(acc4)
    acc1[...] = jnp.zeros_like(acc1)
    blank = jnp.zeros((CH, ny * LANES), BF16)

    @pl.loop(0, nx)
    def _(x):
        acc2[...] += contract(
            line(g3, x, 0, ny),
            jnp.concatenate(neighbour_lines(a1, x + 7, 7, ny) + [blank], axis=0),
        )
        acc4[...] += contract(
            line(f2, x + HALO, HALO, ny),
            jnp.concatenate(neighbour_lines(sk, x + 1, 1, ny) + [blank], axis=0),
        )
        acc1[...] += contract(
            jnp.concatenate(neighbour_lines(f1, x + HALO, HALO, ny), axis=0),
            jnp.concatenate([line(g1, x, 0, ny), blank], axis=0),
        )

    blank = jnp.zeros((CH, cy * LANES), BF16)
    for x in range(cx):
        acc3[...] += contract(
            line(c3, x, 0, cy),
            jnp.concatenate(neighbour_lines(ci, x + 3, 3, cy) + [blank], axis=0),
        )

    for tap in range(27):
        grads_ref[32 * tap : 32 * (tap + 1)] = tap_rows(acc2, tap).astype(BF16)
        grads_ref[864 + 32 * tap : 896 + 32 * tap] = (tap_rows(acc3, tap) * 0.5).astype(BF16)
    for k in range(5):
        grads_ref[1728 + 16 * k : 1744 + 16 * k] = acc4[:, LANES * k : LANES * (k + 1)].astype(
            BF16
        )
    grads_ref[1808:1952] = acc1[...].astype(BF16)
    grads_ref[1952:] = jnp.zeros((96, LANES), BF16)


def unpack_kernel(total_ref, two_ref, three_ref, wide):
    wide[...] = total_ref[:1728].astype(F32)
    for half in range(32):
        lanes = slice(LANES * half, LANES * (half + 1))
        two_ref[:, lanes] = wide[pl.ds(half, 27, stride=32)]
        three_ref[:, lanes] = wide[pl.ds(864 + half, 27, stride=32)]


def in_vmem(count):
    return [pl.BlockSpec(memory_space=pltpu.VMEM)] * count


def body(field_in, cotangent, kernel_one, kernel_two, kernel_three, kernel_four):
    nx, ny, nz = field_in.shape[1:]
    devices = lax.axis_size("gx") * lax.axis_size("gy")
    scale = 1.0 / math.sqrt(nx * ny * nz * devices)

    blank = jnp.zeros((1, nx, ny, nz), BF16)
    block = jnp.concatenate([field_in, blank, cotangent, blank], axis=0)
    block = jnp.transpose(block, (1, 2, 0, 3))
    block = jnp.concatenate(
        [
            shifted(block, "gx", 2),
            shifted(block, "gx", 1),
            block,
            shifted(block, "gx", -1),
            shifted(block, "gx", -2),
        ],
        axis=0,
    )
    block, kernel_one, kernel_two, kernel_three, kernel_four = lax.optimization_barrier(
        (block, kernel_one, kernel_two, kernel_three, kernel_four)
    )
    block = jnp.concatenate(
        [shifted(block, "gy", 1), block, shifted(block, "gy", -1)], axis=1
    )

    t2, t2b, t3, t3b = pl.pallas_call(
        weights_kernel,
        out_shape=[jax.ShapeDtypeStruct((6 * CH, 12 * CH), BF16)] * 4,
        in_specs=in_vmem(2),
        out_specs=in_vmem(4),
        cost_estimate=pl.CostEstimate(flops=0, bytes_accessed=30_000_000, transcendentals=0),
    )(kernel_two.reshape(27, CH, CH), kernel_three.reshape(27, CH, CH))
    four = jnp.transpose(kernel_four, (2, 3, 4, 0, 1))
    weights = (
        toeplitz_window(jnp.transpose(kernel_one, (0, 2, 3, 4, 1))),
        t2,
        t2b,
        t3,
        t3b,
        toeplitz_rows(jnp.pad(four, ((0, 0), (0, 0), (0, 0), (0, 5), (0, 0)))),
        toeplitz_window(jnp.transpose(swapped(four), (3, 0, 1, 2, 4))),
    )

    wide, tall = nx + 2 * HALO, ny + 2 * HALO
    cx, cy = nx // 2, ny // 2

    def fine(more, kind, rows=CH):
        return pltpu.VMEM((nx + 2 * more, ny + 2 * more, rows, LANES), kind)

    def coarse(more, kind, rows=CH):
        return pltpu.VMEM((cx + 2 * more, cy + 2 * more, rows, LANES), kind)

    out, grads = pl.pallas_call(
        lambda *refs: step_kernel(scale, nx, ny, *refs),
        out_shape=[
            jax.ShapeDtypeStruct((nx, ny, 8, LANES), F32),
            jax.ShapeDtypeStruct((2048, LANES), BF16),
        ],
        in_specs=in_vmem(8),
        out_specs=in_vmem(2),
        scratch_shapes=[
            fine(HALO, BF16, 16),
            fine(HALO, BF16, 16),
            fine(7, BF16),
            pltpu.VMEM((nx + 14, ny, CH, LANES), F32),
            fine(6, BF16),
            fine(6, F32),
            fine(4, F32),
            coarse(3, BF16),
            coarse(2, BF16),
            coarse(2, BF16),
            coarse(1, F32),
            fine(1, BF16),
            fine(1, BF16),
            fine(0, BF16, 3 * CH),
            coarse(0, BF16, 3 * CH),
            fine(0, BF16),
            pltpu.VMEM((3 * CH, 640), F32),
            pltpu.VMEM((3 * CH, 640), F32),
            pltpu.VMEM((16, 640), F32),
            pltpu.VMEM((144, LANES), F32),
            pltpu.VMEM((6 * CH, 4 * LANES), F32),
            pltpu.VMEM((6 * CH, 4 * LANES), F32),
        ],
        compiler_params=pltpu.CompilerParams(vmem_limit_bytes=60 * 1024 * 1024),
    )(block, *weights)

    output = jnp.transpose(out[:, :, :3], (2, 0, 1, 3))

    share = lax.all_to_all(grads.reshape(devices, -1, LANES), AXES, 0, 0, tiled=True)
    total = jnp.sum(share.astype(F32), axis=0).astype(BF16)
    total = jnp.broadcast_to(total[None], (devices,) + total.shape)
    total = lax.all_to_all(total, AXES, 0, 0, tiled=True).reshape(2048, LANES)

    grad_two, grad_three = pl.pallas_call(
        unpack_kernel,
        out_shape=[jax.ShapeDtypeStruct((27, CH * CH), F32)] * 2,
        in_specs=in_vmem(1),
        out_specs=in_vmem(2),
        scratch_shapes=[pltpu.VMEM((1728, LANES), F32)],
    )(total)
    last = jnp.concatenate(
        [total[1728 + 16 * k : 1744 + 16 * k] for k in range(5)], axis=1
    )[:12, : 9 * CH].reshape(3, 4, 3, 3, CH)[::-1, :3]
    grad_four = jnp.transpose(last, (1, 4, 2, 3, 0)).astype(F32)
    first = total[1808:1952, :CH].reshape(3, 3, 4, 4, CH)[:, :, :3, :3]
    grad_one = jnp.transpose(first, (4, 3, 0, 1, 2)).astype(F32)
    return (output, grad_one, grad_two, grad_three, grad_four)


def solution(mesh):
    return jax.shard_map(
        body,
        mesh=mesh,
        in_specs=(P(None, "gx", "gy", None), P(None, "gx", "gy", None), P(), P(), P(), P()),
        out_specs=(P(None, "gx", "gy", None), P(), P(), P(), P()),
        check_vma=False,
    )
```

```python
import math

import jax
import jax.numpy as jnp
from jax import lax
from jax.experimental import pallas as pl
from jax.experimental.pallas import tpu as pltpu
from jax.sharding import PartitionSpec as P

F32 = jnp.float32
BF16 = jnp.bfloat16
AXES = ("gx", "gy")
HALO = 8
CH = 64
LANES = 128
FIELD_ROWS = (0, 2, 1, None)
GRADIENT_ROWS = (0, 2, None, 1)


def shifted(block, axis, steps):
    count = lax.axis_size(axis)
    return lax.ppermute(block, axis, [(i, (i + steps) % count) for i in range(count)])


def toeplitz_rows(taps):
    low = jnp.pad(taps, ((0, 0), (0, 1), (0, 0), (0, 0), (0, 0)))
    high = jnp.pad(taps, ((0, 0), (1, 0), (0, 0), (0, 0), (0, 0)))
    both = jnp.stack([low, high])
    both = jnp.transpose(both, (0, 3, 4, 1, 2, 5))
    return both.reshape(6 * taps.shape[3], 12 * taps.shape[4])


def weights_kernel(two_ref, three_ref, t2_ref, t2b_ref, t3_ref, t3b_ref):
    row, column = (lax.broadcasted_iota(jnp.int32, (CH, CH), axis) for axis in range(2))
    eye = (row == column).astype(BF16)
    zero = jnp.zeros((CH, CH), BF16)
    for source, forward, backward in (
        (two_ref, t2_ref, t2b_ref),
        (three_ref, t3_ref, t3b_ref),
    ):
        for a in range(3):
            for e in range(3):
                taps = [source[9 * a + 3 * b + e] for b in range(3)]
                plain = jnp.concatenate([tap.astype(F32) for tap in taps + [zero]], axis=1)
                turn = contract(eye, jnp.concatenate(taps[::-1] + [zero], axis=0))
                for target, values, at, lane in (
                    (forward, plain, CH * e, 4 * CH * a),
                    (backward, turn, CH * (2 - e), 4 * CH * (2 - a)),
                ):
                    lanes = slice(lane, lane + 4 * CH)
                    target[at : at + CH, lanes] = values.astype(BF16)
                    moved = pltpu.roll(values, CH, 1).astype(BF16)
                    target[at + 3 * CH : at + 4 * CH, lanes] = moved


def toeplitz_window(taps, places):
    taps = jnp.pad(taps, ((0, 0),) * 4 + ((0, 1),))
    zero = jnp.zeros_like(taps[:, :, :, 0])
    taps = jnp.concatenate([zero if e is None else taps[:, :, :, e] for e in places], axis=3)
    rows = [
        jnp.pad(taps, ((0, 0), (dx, 1 - dx), (dy, 1 - dy), (0, 0)))
        for dx in range(2)
        for dy in range(2)
    ]
    return jnp.stack(rows).reshape(4 * taps.shape[0], 256)


def swapped(taps):
    return jnp.swapaxes(jnp.flip(taps, (0, 1, 2)), 3, 4)


def leaky(values):
    return values * (0.55 + 0.45 * jnp.tanh(0.5 * values))


def slope(values):
    sigma = 0.5 + 0.5 * jnp.tanh(0.5 * values)
    return 0.1 + 0.9 * sigma * (1.0 + values * (1.0 - sigma))


def turned(values, steps):
    return pltpu.roll(values, steps % LANES, values.ndim - 1)


def window_of(source, x, y):
    rows = [source[x + r, pl.ds(y, 4)].reshape(4 * CH, LANES) for r in range(4)]
    return jnp.concatenate(
        [jnp.concatenate([rows[a], rows[a + 1]], axis=1) for a in range(3)], axis=0
    )


def product_pair(source, weights, x, y):
    window = jnp.concatenate([window_of(source, x, y), window_of(source, x, y + 2)], axis=1)
    return jnp.dot(weights[...], window, preferred_element_type=F32)


def column_of(product, dx, dy, step):
    out = product.shape[0] // 6
    rows, lane = 3 * out * (dy % 2), LANES * (dx + 2 * (dy // 2))
    first, second, third = (
        product[rows + out * e : rows + out * (e + 1), lane : lane + LANES] for e in range(3)
    )
    return turned(first, step) + second + turned(third, -step)


def pipelined(count, most, product, finish, even, odd):
    odd[...] = jnp.zeros(odd.shape, odd.dtype)
    pairs = count // 2
    many = next(m for m in range(most, 0, -1) if pairs % m == 0)

    @pl.loop(0, pairs // many)
    def _(v):
        for w in range(many):
            t = 2 * (v * many + w)
            even[...] = product(t)
            finish(jnp.maximum(t - 1, 0) if w == 0 else t - 1, odd)
            odd[...] = product(t + 1)
            finish(t, even)

    if count % 2:
        even[...] = product(count - 1)
        finish(count - 2, odd)
        finish(count - 1, even)
    else:
        finish(count - 1, odd)


def window_row(source, weights, x, y, blocks):
    parts = []
    for k in range(blocks):
        rows = [source[x + r, pl.ds(y + 2 * k, 4)].reshape(64, LANES) for r in range(4)]
        parts.append(jnp.concatenate(rows, axis=0))
    return jnp.dot(weights[...], jnp.concatenate(parts, axis=1), preferred_element_type=F32)


def window_column(product, dx, y):
    at, lane = CH * (2 * dx + y % 2), LANES * (y // 2)
    return product[at : at + CH, lane : lane + LANES]


def line(source, x, y, count):
    return jnp.concatenate([source[x, y + k] for k in range(count)], axis=1)


def neighbour_lines(source, x, y, count):
    return [line(source, x + a - 1, y + b - 1, count) for a in range(3) for b in range(3)]


def contract(left, right):
    return lax.dot_general(left, right, (((1,), (1,)), ((), ())), preferred_element_type=F32)


def upright(total):
    count = total.shape[1]
    row, column = (lax.broadcasted_iota(jnp.int32, (count, count), axis) for axis in range(2))
    total = jnp.concatenate([total.astype(BF16), jnp.zeros((CH, count), BF16)], axis=0)
    return contract((row == column).astype(BF16), total)


def three_taps(value, step):
    return jnp.concatenate([turned(value, -step), value, turned(value, step)], axis=0).astype(BF16)


def tap_rows(total, tap):
    place, e = tap // 3, tap % 3
    tile = slice(LANES * (place // 2), LANES * (place // 2 + 1))
    even = total[CH * e : CH * e + 32, tile]
    odd = total[CH * e + 32 : CH * (e + 1), tile]
    left = lax.broadcasted_iota(jnp.int32, even.shape, 1) < CH
    if place % 2 == 0:
        return jnp.where(left, even, turned(odd, CH))
    return jnp.where(left, turned(even, CH), odd)


def pair_sum(values):
    lane = lax.broadcasted_iota(jnp.int32, values.shape, 1)
    return values + jnp.where(lane % 2 == 0, turned(values, -1), turned(values, 1))


def step_kernel(
    scale,
    nx,
    ny,
    low_ref,
    own_ref,
    high_ref,
    t1_ref,
    t2_ref,
    t2b_ref,
    t3_ref,
    t3b_ref,
    t4_ref,
    t4b_ref,
    out_ref,
    grads_ref,
    f1,
    f2,
    a1,
    p1,
    a2,
    p2,
    sg,
    ci,
    ca,
    cg,
    pg,
    sk,
    g2,
    g3,
    c3,
    g1,
    acc2,
    acc4,
    acc1,
    even,
    odd,
    even1,
    odd1,
):
    wide, tall = nx + 2 * HALO, ny + 2 * HALO

    @pl.loop(0, wide)
    def _(x):
        cells = jnp.concatenate([low_ref[x], own_ref[x], high_ref[x]], axis=0).astype(F32)
        first = lax.broadcasted_iota(jnp.int32, cells.shape, 1) < 4
        before, after = turned(cells, 1), turned(cells, -1)
        top = jnp.where(first, before, pltpu.roll(after, 4, 1))
        f1[x] = jnp.concatenate([top, cells], axis=1).astype(BF16)
        top = jnp.where(first, pltpu.roll(before, 4, 1), after)
        f2[x] = (jnp.concatenate([top, cells], axis=1) * scale).astype(BF16)

    skip_blocks = (ny + 8) // 2

    def skip_product(i):
        return window_row(f2, t4b_ref, 2 * i + 3, 3, skip_blocks)

    def skip_finish(i, product):
        for dx in range(2):
            for y in range(ny + 8):
                sg[2 * i + dx, y] = window_column(product, dx, y)

    lanes = skip_blocks * LANES
    pipelined((nx + 8) // 2, 1, skip_product, skip_finish, even1.at[:, :lanes], odd1.at[:, :lanes])

    def first_product(i):
        return window_row(f1, t1_ref, 2 * i, 0, (ny + 14) // 2)

    def first_finish(i, product):
        for dx in range(2):
            for y in range(ny + 14):
                value = window_column(product, dx, y)
                a1[2 * i + dx, y] = leaky(value).astype(BF16)
                if 0 <= y - 7 < ny:
                    p1[2 * i + dx, y - 7] = value

    pipelined((nx + 14) // 2, 2, first_product, first_finish, even1, odd1)

    pairs = (ny + 12) // 4

    def second_product(t):
        return product_pair(a1, t2_ref, 2 * (t // pairs), 4 * (t % pairs))

    def second_finish(t, product):
        i, j = t // pairs, t % pairs
        for half in range(2):
            total = None
            for dx in range(2):
                for dy in range(2):
                    value = column_of(product, dx, 2 * half + dy, 1)
                    x, y = 2 * i + dx, 4 * j + 2 * half + dy
                    act = leaky(value).astype(BF16)
                    p2[x, y] = value
                    a2[x, y] = act
                    act = act.astype(F32)
                    total = act if total is None else total + act
            ci[i, 2 * j + half] = (pair_sum(total) * 0.125).astype(BF16)

    pipelined((nx + 12) // 2 * pairs, 5, second_product, second_finish, even, odd)

    cx, cy = nx // 2, ny // 2
    coarse_pairs = (cy + 4) // 4

    def coarse_product(t):
        return product_pair(ci, t3_ref, 2 * (t // coarse_pairs), 4 * (t % coarse_pairs))

    def coarse_finish(t, product):
        for dx in range(2):
            for dy in range(4):
                value = column_of(product, dx, dy, 2)
                x, y = 2 * (t // coarse_pairs) + dx, 4 * (t % coarse_pairs) + dy
                ca[x, y] = leaky(value).astype(BF16)
                total = (
                    sg[2 * x, 2 * y]
                    + sg[2 * x, 2 * y + 1]
                    + sg[2 * x + 1, 2 * y]
                    + sg[2 * x + 1, 2 * y + 1]
                )
                cg[x, y] = (pair_sum(total) * slope(value)).astype(BF16)

    pipelined((cx + 4) // 2 * coarse_pairs, 3, coarse_product, coarse_finish, even, odd)

    @pl.loop(0, (cx + 2) // 2)
    def _(i):
        blocks = (cy + 2) // 2
        window = jnp.concatenate([window_of(cg, 2 * i, 2 * j) for j in range(blocks)], axis=1)
        product = jnp.dot(t3b_ref[...], window, preferred_element_type=F32)
        for dx in range(2):
            for dy in range(2 * blocks):
                pg[2 * i + dx, dy] = column_of(product, dx, dy, 2)

    @pl.loop(0, nx + 2)
    def _(x):
        up = (x + 1) // 2
        for y in range(ny + 2):
            right = (y + 1) // 2
            sk[x, y] = (
                a2[x + 5, y + 5].astype(F32) + ca[up + 1, right + 1].astype(F32)
            ).astype(BF16)
            g2[x, y] = (
                (sg[x + 3, y + 3] + pg[up, right] * 0.125) * slope(p2[x + 5, y + 5])
            ).astype(BF16)

    row, column = (lax.broadcasted_iota(jnp.int32, (CH, CH), axis) for axis in range(2))
    parity = (column == 2 * (row % 32) + row // 32).astype(BF16)

    @pl.loop(0, nx)
    def _(x):
        values = jnp.dot(parity, line(g2, x + 1, 1, ny), preferred_element_type=F32)
        for y in range(ny):
            value = values[:, LANES * y : LANES * (y + 1)]
            g3[x, y] = three_taps(value, 1)

    for x in range(cx):
        values = jnp.dot(parity, line(cg, x + 2, 2, cy), preferred_element_type=F32)
        for y in range(cy):
            c3[x, y] = three_taps(values[:, LANES * y : LANES * (y + 1)], 2)

    @pl.loop(0, nx // 2)
    def _(i):
        blocks = ny // 2
        window = jnp.concatenate([window_of(sk, 2 * i, 2 * j) for j in range(blocks)], axis=1)
        product = jnp.dot(t4_ref[...], window, preferred_element_type=F32)
        for dx in range(2):
            for dy in range(ny):
                x = 2 * i + dx
                out_ref[x, dy] = column_of(product, dx, dy, 1) + own_ref[x + HALO, dy].astype(F32)

    fine_pairs = ny // 4

    def back_product(t):
        return product_pair(g2, t2b_ref, 2 * (t // fine_pairs), 4 * (t % fine_pairs))

    def back_finish(t, product):
        for dx in range(2):
            for dy in range(4):
                x, y = 2 * (t // fine_pairs) + dx, 4 * (t % fine_pairs) + dy
                value = column_of(product, dx, dy, 1)
                g1[x, y] = (value * slope(p1[x + 7, y])).astype(BF16)

    pipelined(nx // 2 * fine_pairs, 2, back_product, back_finish, even, odd)

    acc2[...] = jnp.zeros_like(acc2)
    acc4[...] = jnp.zeros_like(acc4)
    acc1[...] = jnp.zeros_like(acc1)

    @pl.loop(0, nx)
    def _(x):
        acc2[...] += contract(
            jnp.concatenate(neighbour_lines(a1, x + 7, 7, ny), axis=0), line(g3, x, 0, ny)
        )
        acc4[...] += contract(
            jnp.concatenate(neighbour_lines(sk, x + 1, 1, ny), axis=0),
            line(f2, x + HALO, HALO, ny),
        )
        acc1[...] += contract(
            jnp.concatenate(neighbour_lines(f1, x + HALO, HALO, ny), axis=0), line(g1, x, 0, ny)
        )

    total3 = 0.5 * sum(
        contract(jnp.concatenate(neighbour_lines(ci, x + 3, 3, cy), axis=0), line(c3, x, 0, cy))
        for x in range(cx)
    )
    total2, total3, total4 = (
        upright(total) for total in (acc2[...], total3, acc4[...])
    )
    for tap in range(27):
        grads_ref[32 * tap : 32 * (tap + 1)] = tap_rows(total2, tap).astype(BF16)
        grads_ref[864 + 32 * tap : 896 + 32 * tap] = tap_rows(total3, tap).astype(BF16)
    for k in range(5):
        grads_ref[1728 + 16 * k : 1744 + 16 * k] = total4[
            :, LANES * k : LANES * (k + 1)
        ].astype(BF16)
    grads_ref[1808:1952] = jnp.concatenate([acc1[...], jnp.zeros_like(acc1)], axis=1).astype(BF16)
    grads_ref[1952:] = jnp.zeros((96, LANES), BF16)


def unpack_kernel(total_ref, two_ref, three_ref, last_ref, first_ref, wide):
    wide[...] = total_ref[:1728].astype(F32)
    for half in range(32):
        lanes = slice(LANES * half, LANES * (half + 1))
        two_ref[:, lanes] = wide[pl.ds(half, 27, stride=32)]
        three_ref[:, lanes] = wide[pl.ds(864 + half, 27, stride=32)]
    for k in range(5):
        last_ref[:, LANES * k : LANES * (k + 1)] = total_ref[
            1728 + 16 * k : 1744 + 16 * k
        ].astype(F32)
    first_ref[...] = total_ref[1808:1952].astype(F32)


def in_vmem(count):
    return [pl.BlockSpec(memory_space=pltpu.VMEM)] * count


def body(field_in, cotangent, kernel_one, kernel_two, kernel_three, kernel_four):
    nx, ny, nz = field_in.shape[1:]
    devices = lax.axis_size("gx") * lax.axis_size("gy")
    scale = 1.0 / math.sqrt(nx * ny * nz * devices)

    blank = jnp.zeros((1, nx, ny, nz), BF16)
    block = jnp.concatenate([field_in, blank, cotangent, blank], axis=0)
    block = jnp.transpose(block, (1, 2, 0, 3))
    block = jnp.concatenate(
        [
            shifted(block, "gx", 2),
            shifted(block, "gx", 1),
            block,
            shifted(block, "gx", -1),
            shifted(block, "gx", -2),
        ],
        axis=0,
    )
    block, kernel_one, kernel_two, kernel_three, kernel_four = lax.optimization_barrier(
        (block, kernel_one, kernel_two, kernel_three, kernel_four)
    )
    blocks = (shifted(block, "gy", 1), block, shifted(block, "gy", -1))

    t2, t2b, t3, t3b = pl.pallas_call(
        weights_kernel,
        out_shape=[jax.ShapeDtypeStruct((6 * CH, 12 * CH), BF16)] * 4,
        in_specs=in_vmem(2),
        out_specs=in_vmem(4),
        cost_estimate=pl.CostEstimate(flops=0, bytes_accessed=30_000_000, transcendentals=0),
    )(kernel_two.reshape(27, CH, CH), kernel_three.reshape(27, CH, CH))
    four = jnp.transpose(kernel_four, (2, 3, 4, 0, 1))
    weights = (
        toeplitz_window(jnp.transpose(kernel_one, (0, 2, 3, 4, 1)), FIELD_ROWS),
        t2,
        t2b,
        t3,
        t3b,
        toeplitz_rows(jnp.pad(four, ((0, 0), (0, 0), (0, 0), (0, 5), (0, 0)))),
        toeplitz_window(jnp.transpose(swapped(four), (3, 0, 1, 2, 4)), GRADIENT_ROWS),
    )

    wide, tall = nx + 2 * HALO, ny + 2 * HALO
    cx, cy = nx // 2, ny // 2

    def fine(more, kind, rows=CH):
        return pltpu.VMEM((nx + 2 * more, ny + 2 * more, rows, LANES), kind)

    def coarse(more, kind, rows=CH):
        return pltpu.VMEM((cx + 2 * more, cy + 2 * more, rows, LANES), kind)

    out, grads = pl.pallas_call(
        lambda *refs: step_kernel(scale, nx, ny, *refs),
        out_shape=[
            jax.ShapeDtypeStruct((nx, ny, 8, LANES), F32),
            jax.ShapeDtypeStruct((2048, LANES), BF16),
        ],
        in_specs=in_vmem(10),
        out_specs=in_vmem(2),
        scratch_shapes=[
            fine(HALO, BF16, 16),
            fine(HALO, BF16, 16),
            fine(7, BF16),
            pltpu.VMEM((nx + 14, ny, CH, LANES), F32),
            fine(6, BF16),
            fine(6, F32),
            fine(4, F32),
            coarse(3, BF16),
            coarse(2, BF16),
            coarse(2, BF16),
            coarse(1, F32),
            fine(1, BF16),
            fine(1, BF16),
            fine(0, BF16, 3 * CH),
            coarse(0, BF16, 3 * CH),
            fine(0, BF16),
            pltpu.VMEM((9 * CH, 3 * CH), F32),
            pltpu.VMEM((9 * CH, 16), F32),
            pltpu.VMEM((144, CH), F32),
            pltpu.VMEM((6 * CH, 4 * LANES), F32),
            pltpu.VMEM((6 * CH, 4 * LANES), F32),
            pltpu.VMEM((4 * CH, (ny + 14) // 2 * LANES), F32),
            pltpu.VMEM((4 * CH, (ny + 14) // 2 * LANES), F32),
        ],
        compiler_params=pltpu.CompilerParams(vmem_limit_bytes=60 * 1024 * 1024),
    )(*blocks, *weights)

    output = jnp.transpose(out[:, :, :3], (2, 0, 1, 3))

    share = lax.all_to_all(grads.reshape(devices, -1, LANES), AXES, 0, 0, tiled=True)
    total = jnp.sum(share.astype(F32), axis=0).astype(BF16)
    total = jnp.broadcast_to(total[None], (devices,) + total.shape)
    total = lax.all_to_all(total, AXES, 0, 0, tiled=True).reshape(2048, LANES)

    grad_two, grad_three, last, first = pl.pallas_call(
        unpack_kernel,
        out_shape=[jax.ShapeDtypeStruct((27, CH * CH), F32)] * 2
        + [
            jax.ShapeDtypeStruct((16, 5 * LANES), F32),
            jax.ShapeDtypeStruct((144, LANES), F32),
        ],
        in_specs=in_vmem(1),
        out_specs=in_vmem(4),
        scratch_shapes=[pltpu.VMEM((1728, LANES), F32)],
    )(total)
    groups = [last[4 * k : 4 * k + 3, : 9 * CH] for k in range(4)]
    taps = [groups[GRADIENT_ROWS.index(2 - e)] for e in range(3)]
    taps = jnp.stack(taps, axis=2).reshape(3, 3, 3, CH, 3)
    grad_four = jnp.transpose(taps, (0, 3, 1, 2, 4))
    first = first[:, :CH].reshape(3, 3, 4, 4, CH)
    taps = jnp.stack([first[:, :, FIELD_ROWS.index(e), :3] for e in range(3)], axis=2)
    grad_one = jnp.transpose(taps, (4, 3, 0, 1, 2))
    return (output, grad_one, grad_two, grad_three, grad_four)


def solution(mesh):
    return jax.shard_map(
        body,
        mesh=mesh,
        in_specs=(P(None, "gx", "gy", None), P(None, "gx", "gy", None), P(), P(), P(), P()),
        out_specs=(P(None, "gx", "gy", None), P(), P(), P(), P()),
        check_vma=False,
    )
```

```python
import math

import jax
import jax.numpy as jnp
from jax import lax
from jax.experimental import pallas as pl
from jax.experimental.pallas import tpu as pltpu
from jax.sharding import PartitionSpec as P

F32 = jnp.float32
BF16 = jnp.bfloat16
AXES = ("gx", "gy")
HALO = 8
CH = 64
LANES = 128
FIELD_ROWS = (0, 2, 1, None)
GRADIENT_ROWS = (0, 2, None, 1)


def shifted(block, axis, steps):
    count = lax.axis_size(axis)
    return lax.ppermute(block, axis, [(i, (i + steps) % count) for i in range(count)])


def toeplitz_rows(taps):
    low = jnp.pad(taps, ((0, 0), (0, 1), (0, 0), (0, 0), (0, 0)))
    high = jnp.pad(taps, ((0, 0), (1, 0), (0, 0), (0, 0), (0, 0)))
    both = jnp.stack([low, high])
    both = jnp.transpose(both, (0, 3, 4, 1, 2, 5))
    return both.reshape(6 * taps.shape[3], 12 * taps.shape[4])


def weights_kernel(two_ref, three_ref, t2_ref, t2b_ref, t3_ref, t3b_ref):
    row, column = (lax.broadcasted_iota(jnp.int32, (CH, CH), axis) for axis in range(2))
    eye = (row == column).astype(BF16)
    zero = jnp.zeros((CH, CH), BF16)
    for source, forward, backward in (
        (two_ref, t2_ref, t2b_ref),
        (three_ref, t3_ref, t3b_ref),
    ):
        for a in range(3):
            for e in range(3):
                taps = [source[9 * a + 3 * b + e] for b in range(3)]
                plain = jnp.concatenate([tap.astype(F32) for tap in taps + [zero]], axis=1)
                turn = contract(eye, jnp.concatenate(taps[::-1] + [zero], axis=0))
                for target, values, at, lane in (
                    (forward, plain, CH * e, 4 * CH * a),
                    (backward, turn, CH * (2 - e), 4 * CH * (2 - a)),
                ):
                    lanes = slice(lane, lane + 4 * CH)
                    target[at : at + CH, lanes] = values.astype(BF16)
                    moved = pltpu.roll(values, CH, 1).astype(BF16)
                    target[at + 3 * CH : at + 4 * CH, lanes] = moved


def toeplitz_window(taps, places):
    taps = jnp.pad(taps, ((0, 0),) * 4 + ((0, 1),))
    zero = jnp.zeros_like(taps[:, :, :, 0])
    taps = jnp.concatenate([zero if e is None else taps[:, :, :, e] for e in places], axis=3)
    rows = [
        jnp.pad(taps, ((0, 0), (dx, 1 - dx), (dy, 1 - dy), (0, 0)))
        for dx in range(2)
        for dy in range(2)
    ]
    return jnp.stack(rows).reshape(4 * taps.shape[0], 256)


def swapped(taps):
    return jnp.swapaxes(jnp.flip(taps, (0, 1, 2)), 3, 4)


def leaky(values):
    return values * (0.55 + 0.45 * jnp.tanh(0.5 * values))


def slope(values):
    sigma = 0.5 + 0.5 * jnp.tanh(0.5 * values)
    return 0.1 + 0.9 * sigma * (1.0 + values * (1.0 - sigma))


def turned(values, steps):
    return pltpu.roll(values, steps % LANES, values.ndim - 1)


def window_of(source, x, y):
    rows = [source[x + r, pl.ds(y, 4)].reshape(4 * CH, LANES) for r in range(4)]
    return jnp.concatenate(
        [jnp.concatenate([rows[a], rows[a + 1]], axis=1) for a in range(3)], axis=0
    )


def product_pair(source, weights, x, y):
    window = jnp.concatenate([window_of(source, x, y), window_of(source, x, y + 2)], axis=1)
    return jnp.dot(weights[...], window, preferred_element_type=F32)


def column_of(product, dx, dy, step):
    out = product.shape[0] // 6
    rows, lane = 3 * out * (dy % 2), LANES * (dx + 2 * (dy // 2))
    first, second, third = (
        product[rows + out * e : rows + out * (e + 1), lane : lane + LANES] for e in range(3)
    )
    return turned(first, step) + second + turned(third, -step)


def pipelined(count, most, product, finish, even, odd):
    odd[...] = jnp.zeros(odd.shape, odd.dtype)
    pairs = count // 2
    many = next(m for m in range(most, 0, -1) if pairs % m == 0)

    @pl.loop(0, pairs // many)
    def _(v):
        for w in range(many):
            t = 2 * (v * many + w)
            even[...] = product(t)
            finish(jnp.maximum(t - 1, 0) if w == 0 else t - 1, odd)
            odd[...] = product(t + 1)
            finish(t, even)

    if count % 2:
        even[...] = product(count - 1)
        finish(count - 2, odd)
        finish(count - 1, even)
    else:
        finish(count - 1, odd)


def window_row(source, weights, x, y, blocks):
    parts = []
    for k in range(blocks):
        rows = [source[x + r, pl.ds(y + 2 * k, 4)].reshape(64, LANES) for r in range(4)]
        parts.append(jnp.concatenate(rows, axis=0))
    return jnp.dot(weights[...], jnp.concatenate(parts, axis=1), preferred_element_type=F32)


def window_column(product, dx, y):
    at, lane = CH * (2 * dx + y % 2), LANES * (y // 2)
    return product[at : at + CH, lane : lane + LANES]


def line(source, x, y, count):
    return jnp.concatenate([source[x, y + k] for k in range(count)], axis=1)


def neighbour_lines(source, x, y, count):
    return [line(source, x + a - 1, y + b - 1, count) for a in range(3) for b in range(3)]


def contract(left, right):
    return lax.dot_general(left, right, (((1,), (1,)), ((), ())), preferred_element_type=F32)


def upright(total):
    count = total.shape[1]
    row, column = (lax.broadcasted_iota(jnp.int32, (count, count), axis) for axis in range(2))
    total = jnp.concatenate([total.astype(BF16), jnp.zeros((CH, count), BF16)], axis=0)
    return contract((row == column).astype(BF16), total)


def three_taps(value, step):
    return jnp.concatenate([turned(value, -step), value, turned(value, step)], axis=0).astype(BF16)


def tap_rows(total, tap):
    place, e = tap // 3, tap % 3
    tile = slice(LANES * (place // 2), LANES * (place // 2 + 1))
    even = total[CH * e : CH * e + 32, tile]
    odd = total[CH * e + 32 : CH * (e + 1), tile]
    left = lax.broadcasted_iota(jnp.int32, even.shape, 1) < CH
    if place % 2 == 0:
        return jnp.where(left, even, turned(odd, CH))
    return jnp.where(left, turned(even, CH), odd)


def pair_sum(values):
    lane = lax.broadcasted_iota(jnp.int32, values.shape, 1)
    return values + jnp.where(lane % 2 == 0, turned(values, -1), turned(values, 1))


def step_kernel(
    scale,
    nx,
    ny,
    below2_ref,
    below1_ref,
    own_ref,
    above1_ref,
    above2_ref,
    t1_ref,
    t2_ref,
    t2b_ref,
    t3_ref,
    t3b_ref,
    t4b_ref,
    sk,
    grads_ref,
    f1,
    f2,
    a1,
    p1,
    a2,
    p2,
    sg,
    ci,
    ca,
    cg,
    pg,
    g2,
    g3,
    c3,
    g1,
    acc2,
    acc4,
    acc1,
    even,
    odd,
    even1,
    odd1,
):
    wide, tall = nx + 2 * HALO, ny + 2 * HALO

    def input_rows(part, first_x):
        @pl.loop(0, nx, unroll=2)
        def _(x):
            cells = part[x].astype(F32)
            first = lax.broadcasted_iota(jnp.int32, cells.shape, 1) < 4
            before, after = turned(cells, 1), turned(cells, -1)
            top = jnp.where(first, before, pltpu.roll(after, 4, 1))
            f1[x + first_x] = jnp.concatenate([top, cells], axis=1).astype(BF16)
            top = jnp.where(first, pltpu.roll(before, 4, 1), after)
            f2[x + first_x] = (jnp.concatenate([top, cells], axis=1) * scale).astype(BF16)

    for k, part in enumerate((below2_ref, below1_ref, own_ref, above1_ref, above2_ref)):
        input_rows(part, k * nx)

    skip_blocks = (ny + 8) // 2

    def skip_product(i):
        return window_row(f2, t4b_ref, 2 * i + 3, 3, skip_blocks)

    def skip_finish(i, product):
        for dx in range(2):
            for y in range(ny + 8):
                sg[2 * i + dx, y] = window_column(product, dx, y)

    lanes = skip_blocks * LANES
    pipelined((nx + 8) // 2, 3, skip_product, skip_finish, even1.at[:, :lanes], odd1.at[:, :lanes])

    def first_product(i):
        return window_row(f1, t1_ref, 2 * i, 0, (ny + 14) // 2)

    def first_finish(i, product):
        for dx in range(2):
            for y in range(ny + 14):
                value = window_column(product, dx, y)
                a1[2 * i + dx, y] = leaky(value).astype(BF16)
                if 0 <= y - 7 < ny:
                    p1[2 * i + dx, y - 7] = value

    pipelined((nx + 14) // 2, 2, first_product, first_finish, even1, odd1)

    pairs = (ny + 12) // 4

    def second_product(t):
        return product_pair(a1, t2_ref, 2 * (t // pairs), 4 * (t % pairs))

    def second_finish(t, product):
        i, j = t // pairs, t % pairs
        for half in range(2):
            total = None
            for dx in range(2):
                for dy in range(2):
                    value = column_of(product, dx, 2 * half + dy, 1)
                    x, y = 2 * i + dx, 4 * j + 2 * half + dy
                    act = leaky(value).astype(BF16)
                    p2[x, y] = value
                    a2[x, y] = act
                    act = act.astype(F32)
                    total = act if total is None else total + act
            ci[i, 2 * j + half] = (pair_sum(total) * 0.125).astype(BF16)

    pipelined((nx + 12) // 2 * pairs, 5, second_product, second_finish, even, odd)

    cx, cy = nx // 2, ny // 2
    coarse_pairs = (cy + 4) // 4

    def coarse_product(t):
        return product_pair(ci, t3_ref, 2 * (t // coarse_pairs), 4 * (t % coarse_pairs))

    def coarse_finish(t, product):
        for dx in range(2):
            for dy in range(4):
                value = column_of(product, dx, dy, 2)
                x, y = 2 * (t // coarse_pairs) + dx, 4 * (t % coarse_pairs) + dy
                ca[x, y] = leaky(value).astype(BF16)
                total = (
                    sg[2 * x, 2 * y]
                    + sg[2 * x, 2 * y + 1]
                    + sg[2 * x + 1, 2 * y]
                    + sg[2 * x + 1, 2 * y + 1]
                )
                cg[x, y] = (pair_sum(total) * slope(value)).astype(BF16)

    pipelined((cx + 4) // 2 * coarse_pairs, 3, coarse_product, coarse_finish, even, odd)

    @pl.loop(0, (cx + 2) // 2, unroll=True)
    def _(i):
        blocks = (cy + 2) // 2
        window = jnp.concatenate([window_of(cg, 2 * i, 2 * j) for j in range(blocks)], axis=1)
        product = jnp.dot(t3b_ref[...], window, preferred_element_type=F32)
        for dx in range(2):
            for dy in range(2 * blocks):
                pg[2 * i + dx, dy] = column_of(product, dx, dy, 2)

    @pl.loop(0, nx + 2, unroll=2)
    def _(x):
        up = (x + 1) // 2
        for y in range(ny + 2):
            right = (y + 1) // 2
            sk[x, y] = (
                a2[x + 5, y + 5].astype(F32) + ca[up + 1, right + 1].astype(F32)
            ).astype(BF16)
            g2[x, y] = (
                (sg[x + 3, y + 3] + pg[up, right] * 0.125) * slope(p2[x + 5, y + 5])
            ).astype(BF16)

    row, column = (lax.broadcasted_iota(jnp.int32, (CH, CH), axis) for axis in range(2))
    parity = (column == 2 * (row % 32) + row // 32).astype(BF16)

    @pl.loop(0, nx, unroll=True)
    def _(x):
        values = jnp.dot(parity, line(g2, x + 1, 1, ny), preferred_element_type=F32)
        for y in range(ny):
            value = values[:, LANES * y : LANES * (y + 1)]
            g3[x, y] = three_taps(value, 1)

    for x in range(cx):
        values = jnp.dot(parity, line(cg, x + 2, 2, cy), preferred_element_type=F32)
        for y in range(cy):
            c3[x, y] = three_taps(values[:, LANES * y : LANES * (y + 1)], 2)

    fine_pairs = ny // 4

    def back_product(t):
        return product_pair(g2, t2b_ref, 2 * (t // fine_pairs), 4 * (t % fine_pairs))

    def back_finish(t, product):
        for dx in range(2):
            for dy in range(4):
                x, y = 2 * (t // fine_pairs) + dx, 4 * (t % fine_pairs) + dy
                value = column_of(product, dx, dy, 1)
                g1[x, y] = (value * slope(p1[x + 7, y])).astype(BF16)

    pipelined(nx // 2 * fine_pairs, 2, back_product, back_finish, even, odd)

    acc2[...] = jnp.zeros_like(acc2)
    acc4[...] = jnp.zeros_like(acc4)
    acc1[...] = jnp.zeros_like(acc1)

    @pl.loop(0, nx, unroll=2)
    def _(x):
        acc2[...] += contract(
            jnp.concatenate(neighbour_lines(a1, x + 7, 7, ny), axis=0), line(g3, x, 0, ny)
        )
        acc4[...] += contract(
            jnp.concatenate(neighbour_lines(sk, x + 1, 1, ny), axis=0),
            line(f2, x + HALO, HALO, ny),
        )
        acc1[...] += contract(
            jnp.concatenate(neighbour_lines(f1, x + HALO, HALO, ny), axis=0), line(g1, x, 0, ny)
        )

    total3 = 0.5 * sum(
        contract(jnp.concatenate(neighbour_lines(ci, x + 3, 3, cy), axis=0), line(c3, x, 0, cy))
        for x in range(cx)
    )
    total2, total3, total4 = (
        upright(total) for total in (acc2[...], total3, acc4[...])
    )
    for tap in range(27):
        grads_ref[32 * tap : 32 * (tap + 1)] = tap_rows(total2, tap).astype(BF16)
        grads_ref[864 + 32 * tap : 896 + 32 * tap] = tap_rows(total3, tap).astype(BF16)
    for k in range(5):
        grads_ref[1728 + 16 * k : 1744 + 16 * k] = total4[
            :, LANES * k : LANES * (k + 1)
        ].astype(BF16)
    grads_ref[1808:1952] = jnp.concatenate([acc1[...], jnp.zeros_like(acc1)], axis=1).astype(BF16)
    grads_ref[1952:] = jnp.zeros((96, LANES), BF16)


def output_kernel(sk, own_ref, t4_ref, out_ref):
    nx, ny = own_ref.shape[:2]

    @pl.loop(0, nx // 2)
    def _(i):
        blocks = ny // 2
        window = jnp.concatenate([window_of(sk, 2 * i, 2 * j) for j in range(blocks)], axis=1)
        product = jnp.dot(t4_ref[...], window, preferred_element_type=F32)
        for dx in range(2):
            for y in range(ny):
                x = 2 * i + dx
                out_ref[x, y] = column_of(product, dx, y, 1) + own_ref[x, y].astype(F32)


def unpack_kernel(total_ref, two_ref, three_ref, last_ref, first_ref, wide):
    wide[...] = total_ref[:1728].astype(F32)
    for half in range(32):
        lanes = slice(LANES * half, LANES * (half + 1))
        two_ref[:, lanes] = wide[pl.ds(half, 27, stride=32)]
        three_ref[:, lanes] = wide[pl.ds(864 + half, 27, stride=32)]
    for k in range(5):
        last_ref[:, LANES * k : LANES * (k + 1)] = total_ref[
            1728 + 16 * k : 1744 + 16 * k
        ].astype(F32)
    first_ref[...] = total_ref[1808:1952].astype(F32)


def in_vmem(count):
    return [pl.BlockSpec(memory_space=pltpu.VMEM)] * count


def body(field_in, cotangent, kernel_one, kernel_two, kernel_three, kernel_four):
    nx, ny, nz = field_in.shape[1:]
    devices = lax.axis_size("gx") * lax.axis_size("gy")
    scale = 1.0 / math.sqrt(nx * ny * nz * devices)

    blank = jnp.zeros((1, nx, ny, nz), BF16)
    block = jnp.concatenate([field_in, blank, cotangent, blank], axis=0)
    own = jnp.transpose(block, (1, 2, 0, 3))
    block = jnp.concatenate([shifted(own, "gy", 1), own, shifted(own, "gy", -1)], axis=1)
    block, kernel_two, kernel_three = lax.optimization_barrier(
        (block, kernel_two, kernel_three)
    )
    below2, below1 = shifted(block, "gx", 2), shifted(block, "gx", 1)
    above1, above2 = shifted(block, "gx", -1), shifted(block, "gx", -2)
    blocks = (below2, below1, block, above1, above2)

    t2, t2b, t3, t3b = pl.pallas_call(
        weights_kernel,
        out_shape=[jax.ShapeDtypeStruct((6 * CH, 12 * CH), BF16)] * 4,
        in_specs=in_vmem(2),
        out_specs=in_vmem(4),
        cost_estimate=pl.CostEstimate(flops=0, bytes_accessed=30_000_000, transcendentals=0),
    )(kernel_two.reshape(27, CH, CH), kernel_three.reshape(27, CH, CH))
    four = jnp.transpose(kernel_four, (2, 3, 4, 0, 1))
    weights = (
        toeplitz_window(jnp.transpose(kernel_one, (0, 2, 3, 4, 1)), FIELD_ROWS),
        t2,
        t2b,
        t3,
        t3b,
        toeplitz_window(jnp.transpose(swapped(four), (3, 0, 1, 2, 4)), GRADIENT_ROWS),
    )

    wide, tall = nx + 2 * HALO, ny + 2 * HALO
    cx, cy = nx // 2, ny // 2

    def fine(more, kind, rows=CH):
        return pltpu.VMEM((nx + 2 * more, ny + 2 * more, rows, LANES), kind)

    def coarse(more, kind, rows=CH):
        return pltpu.VMEM((cx + 2 * more, cy + 2 * more, rows, LANES), kind)

    skip_sum, grads = pl.pallas_call(
        lambda *refs: step_kernel(scale, nx, ny, *refs),
        out_shape=[
            jax.ShapeDtypeStruct((nx + 2, ny + 2, CH, LANES), BF16),
            jax.ShapeDtypeStruct((2048, LANES), BF16),
        ],
        in_specs=in_vmem(11),
        out_specs=in_vmem(2),
        scratch_shapes=[
            fine(HALO, BF16, 16),
            fine(HALO, BF16, 16),
            fine(7, BF16),
            pltpu.VMEM((nx + 14, ny, CH, LANES), F32),
            fine(6, BF16),
            fine(6, F32),
            fine(4, F32),
            coarse(3, BF16),
            coarse(2, BF16),
            coarse(2, BF16),
            coarse(1, F32),
            fine(1, BF16),
            fine(0, BF16, 3 * CH),
            coarse(0, BF16, 3 * CH),
            fine(0, BF16),
            pltpu.VMEM((9 * CH, 3 * CH), F32),
            pltpu.VMEM((9 * CH, 16), F32),
            pltpu.VMEM((144, CH), F32),
            pltpu.VMEM((6 * CH, 4 * LANES), F32),
            pltpu.VMEM((6 * CH, 4 * LANES), F32),
            pltpu.VMEM((4 * CH, (ny + 14) // 2 * LANES), F32),
            pltpu.VMEM((4 * CH, (ny + 14) // 2 * LANES), F32),
        ],
        compiler_params=pltpu.CompilerParams(vmem_limit_bytes=60 * 1024 * 1024),
    )(*blocks, *weights)

    t4 = toeplitz_rows(jnp.pad(four, ((0, 0), (0, 0), (0, 0), (0, 5), (0, 0))))
    out = pl.pallas_call(
        output_kernel,
        out_shape=jax.ShapeDtypeStruct((nx, ny, 8, LANES), F32),
        in_specs=in_vmem(3),
        out_specs=in_vmem(1)[0],
        cost_estimate=pl.CostEstimate(
            flops=2 * 48 * 12 * CH * nx * ny * LANES // 2, bytes_accessed=2_000_000, transcendentals=0
        ),
    )(skip_sum, own, t4)
    output = jnp.transpose(out[:, :, :3], (2, 0, 1, 3))

    share = lax.all_to_all(grads.reshape(devices, -1, LANES), AXES, 0, 0, tiled=True)
    total = jnp.sum(share.astype(F32), axis=0).astype(BF16)
    total = jnp.broadcast_to(total[None], (devices,) + total.shape)
    total = lax.all_to_all(total, AXES, 0, 0, tiled=True).reshape(2048, LANES)

    grad_two, grad_three, last, first = pl.pallas_call(
        unpack_kernel,
        out_shape=[jax.ShapeDtypeStruct((27, CH * CH), F32)] * 2
        + [
            jax.ShapeDtypeStruct((16, 5 * LANES), F32),
            jax.ShapeDtypeStruct((144, LANES), F32),
        ],
        in_specs=in_vmem(1),
        out_specs=in_vmem(4),
        scratch_shapes=[pltpu.VMEM((1728, LANES), F32)],
    )(total)
    groups = [last[4 * k : 4 * k + 3, : 9 * CH] for k in range(4)]
    taps = [groups[GRADIENT_ROWS.index(2 - e)] for e in range(3)]
    taps = jnp.stack(taps, axis=2).reshape(3, 3, 3, CH, 3)
    grad_four = jnp.transpose(taps, (0, 3, 1, 2, 4))
    first = first[:, :CH].reshape(3, 3, 4, 4, CH)
    taps = jnp.stack([first[:, :, FIELD_ROWS.index(e), :3] for e in range(3)], axis=2)
    grad_one = jnp.transpose(taps, (4, 3, 0, 1, 2))
    return (output, grad_one, grad_two, grad_three, grad_four)


def solution(mesh):
    return jax.shard_map(
        body,
        mesh=mesh,
        in_specs=(P(None, "gx", "gy", None), P(None, "gx", "gy", None), P(), P(), P(), P()),
        out_specs=(P(None, "gx", "gy", None), P(), P(), P(), P()),
        check_vma=False,
    )
```

```python
import math

import jax
import jax.numpy as jnp
from jax import lax
from jax.experimental import pallas as pl
from jax.experimental.pallas import tpu as pltpu
from jax.sharding import PartitionSpec as P

F32 = jnp.float32
BF16 = jnp.bfloat16
AXES = ("gx", "gy")
HALO = 8
CH = 64
LANES = 128
FIELD_ROWS = (0, 2, 1, None)
GRADIENT_ROWS = (0, 2, None, 1)


def shifted(block, axis, steps):
    count = lax.axis_size(axis)
    return lax.ppermute(block, axis, [(i, (i + steps) % count) for i in range(count)])


def toeplitz_rows(taps):
    low = jnp.pad(taps, ((0, 0), (0, 1), (0, 0), (0, 0), (0, 0)))
    high = jnp.pad(taps, ((0, 0), (1, 0), (0, 0), (0, 0), (0, 0)))
    both = jnp.stack([low, high])
    both = jnp.transpose(both, (0, 3, 4, 1, 2, 5))
    return both.reshape(6 * taps.shape[3], 12 * taps.shape[4])


def weights_kernel(two_ref, three_ref, t2_ref, t2b_ref, t3_ref, t3b_ref):
    row, column = (lax.broadcasted_iota(jnp.int32, (CH, CH), axis) for axis in range(2))
    eye = (row == column).astype(BF16)
    zero = jnp.zeros((CH, CH), BF16)
    for source, forward, backward in (
        (two_ref, t2_ref, t2b_ref),
        (three_ref, t3_ref, t3b_ref),
    ):
        for a in range(3):
            for e in range(3):
                taps = [source[9 * a + 3 * b + e] for b in range(3)]
                plain = jnp.concatenate([tap.astype(F32) for tap in taps + [zero]], axis=1)
                turn = contract(eye, jnp.concatenate(taps[::-1] + [zero], axis=0))
                for target, values, at, lane in (
                    (forward, plain, CH * e, 4 * CH * a),
                    (backward, turn, CH * (2 - e), 4 * CH * (2 - a)),
                ):
                    lanes = slice(lane, lane + 4 * CH)
                    target[at : at + CH, lanes] = values.astype(BF16)
                    moved = pltpu.roll(values, CH, 1).astype(BF16)
                    target[at + 3 * CH : at + 4 * CH, lanes] = moved


def toeplitz_window(taps, places):
    taps = jnp.pad(taps, ((0, 0),) * 4 + ((0, 1),))
    zero = jnp.zeros_like(taps[:, :, :, 0])
    taps = jnp.concatenate([zero if e is None else taps[:, :, :, e] for e in places], axis=3)
    rows = [
        jnp.pad(taps, ((0, 0), (dx, 1 - dx), (dy, 1 - dy), (0, 0)))
        for dx in range(2)
        for dy in range(2)
    ]
    return jnp.stack(rows).reshape(4 * taps.shape[0], 256)


def swapped(taps):
    return jnp.swapaxes(jnp.flip(taps, (0, 1, 2)), 3, 4)


def leaky(values):
    return values * (0.55 + 0.45 * jnp.tanh(0.5 * values))


def slope(values):
    sigma = 0.5 + 0.5 * jnp.tanh(0.5 * values)
    return 0.1 + 0.9 * sigma * (1.0 + values * (1.0 - sigma))


def turned(values, steps):
    return pltpu.roll(values, steps % LANES, values.ndim - 1)


def window_of(source, x, y):
    rows = [source[x + r, pl.ds(y, 4)].reshape(4 * CH, LANES) for r in range(4)]
    return jnp.concatenate(
        [jnp.concatenate([rows[a], rows[a + 1]], axis=1) for a in range(3)], axis=0
    )


def product_pair(source, weights, x, y):
    window = jnp.concatenate([window_of(source, x, y), window_of(source, x, y + 2)], axis=1)
    return jnp.dot(weights[...], window, preferred_element_type=F32)


def column_of(product, dx, dy, step):
    out = product.shape[0] // 6
    rows, lane = 3 * out * (dy % 2), LANES * (dx + 2 * (dy // 2))
    first, second, third = (
        product[rows + out * e : rows + out * (e + 1), lane : lane + LANES] for e in range(3)
    )
    return turned(first, step) + second + turned(third, -step)


def pipelined(count, most, product, finish, even, odd):
    odd[...] = jnp.zeros(odd.shape, odd.dtype)
    pairs = count // 2
    many = next(m for m in range(most, 0, -1) if pairs % m == 0)

    @pl.loop(0, pairs // many)
    def _(v):
        for w in range(many):
            t = 2 * (v * many + w)
            even[...] = product(t)
            finish(jnp.maximum(t - 1, 0) if w == 0 else t - 1, odd)
            odd[...] = product(t + 1)
            finish(t, even)

    if count % 2:
        even[...] = product(count - 1)
        finish(count - 2, odd)
        finish(count - 1, even)
    else:
        finish(count - 1, odd)


def window_row(source, weights, x, y, blocks):
    parts = []
    for k in range(blocks):
        rows = [source[x + r, pl.ds(y + 2 * k, 4)].reshape(64, LANES) for r in range(4)]
        parts.append(jnp.concatenate(rows, axis=0))
    return jnp.dot(weights[...], jnp.concatenate(parts, axis=1), preferred_element_type=F32)


def window_column(product, dx, y):
    at, lane = CH * (2 * dx + y % 2), LANES * (y // 2)
    return product[at : at + CH, lane : lane + LANES]


def line(source, x, y, count):
    return jnp.concatenate([source[x, y + k] for k in range(count)], axis=1)


def neighbour_lines(source, x, y, count):
    return [line(source, x + a - 1, y + b - 1, count) for a in range(3) for b in range(3)]


def contract(left, right):
    return lax.dot_general(left, right, (((1,), (1,)), ((), ())), preferred_element_type=F32)


def upright(total):
    count = total.shape[1]
    row, column = (lax.broadcasted_iota(jnp.int32, (count, count), axis) for axis in range(2))
    total = jnp.concatenate([total.astype(BF16), jnp.zeros((CH, count), BF16)], axis=0)
    return contract((row == column).astype(BF16), total)


def three_taps(value, step):
    return jnp.concatenate([turned(value, -step), value, turned(value, step)], axis=0).astype(BF16)


def tap_rows(total, tap):
    place, e = tap // 3, tap % 3
    tile = slice(LANES * (place // 2), LANES * (place // 2 + 1))
    even = total[CH * e : CH * e + 32, tile]
    odd = total[CH * e + 32 : CH * (e + 1), tile]
    left = lax.broadcasted_iota(jnp.int32, even.shape, 1) < CH
    if place % 2 == 0:
        return jnp.where(left, even, turned(odd, CH))
    return jnp.where(left, turned(even, CH), odd)


def pair_sum(values):
    lane = lax.broadcasted_iota(jnp.int32, values.shape, 1)
    return values + jnp.where(lane % 2 == 0, turned(values, -1), turned(values, 1))


def step_kernel(
    scale,
    nx,
    ny,
    below2_ref,
    below1_ref,
    own_ref,
    above1_ref,
    above2_ref,
    t1_ref,
    t2_ref,
    t2b_ref,
    t3_ref,
    t3b_ref,
    t4b_ref,
    sk,
    grads_ref,
    f1,
    f2,
    a1,
    p1,
    a2,
    p2,
    sg,
    ci,
    ca,
    cg,
    pg,
    g2,
    g3,
    c3,
    g1,
    acc2,
    acc4,
    acc1,
    even,
    odd,
    even1,
    odd1,
):
    wide, tall = nx + 2 * HALO, ny + 2 * HALO

    def input_rows(part, first_x):
        @pl.loop(0, nx, unroll=4)
        def _(x):
            cells = part[x].astype(F32)
            first = lax.broadcasted_iota(jnp.int32, cells.shape, 1) < 4
            before, after = turned(cells, 1), turned(cells, -1)
            top = jnp.where(first, before, pltpu.roll(after, 4, 1))
            f1[x + first_x] = jnp.concatenate([top, cells], axis=1).astype(BF16)
            top = jnp.where(first, pltpu.roll(before, 4, 1), after)
            f2[x + first_x] = (jnp.concatenate([top, cells], axis=1) * scale).astype(BF16)

    for k, part in enumerate((below2_ref, below1_ref, own_ref, above1_ref, above2_ref)):
        input_rows(part, k * nx)

    skip_blocks = (ny + 8) // 2

    def skip_product(i):
        return window_row(f2, t4b_ref, 2 * i + 3, 3, skip_blocks)

    def skip_finish(i, product):
        for dx in range(2):
            for y in range(ny + 8):
                sg[2 * i + dx, y] = window_column(product, dx, y)

    lanes = skip_blocks * LANES
    pipelined((nx + 8) // 2, 3, skip_product, skip_finish, even1.at[:, :lanes], odd1.at[:, :lanes])

    def first_product(i):
        return window_row(f1, t1_ref, 2 * i, 0, (ny + 14) // 2)

    def first_finish(i, product):
        for dx in range(2):
            for y in range(ny + 14):
                value = window_column(product, dx, y)
                a1[2 * i + dx, y] = leaky(value).astype(BF16)
                if 0 <= y - 7 < ny:
                    p1[2 * i + dx, y - 7] = value

    pipelined((nx + 14) // 2, 4, first_product, first_finish, even1, odd1)

    pairs = (ny + 12) // 4

    def second_product(t):
        return product_pair(a1, t2_ref, 2 * (t // pairs), 4 * (t % pairs))

    def second_finish(t, product):
        i, j = t // pairs, t % pairs
        for half in range(2):
            total = None
            for dx in range(2):
                for dy in range(2):
                    value = column_of(product, dx, 2 * half + dy, 1)
                    x, y = 2 * i + dx, 4 * j + 2 * half + dy
                    act = leaky(value).astype(BF16)
                    p2[x, y] = value
                    a2[x, y] = act
                    act = act.astype(F32)
                    total = act if total is None else total + act
            ci[i, 2 * j + half] = (pair_sum(total) * 0.125).astype(BF16)

    pipelined((nx + 12) // 2 * pairs, 5, second_product, second_finish, even, odd)

    cx, cy = nx // 2, ny // 2
    coarse_pairs = (cy + 4) // 4

    def coarse_product(t):
        return product_pair(ci, t3_ref, 2 * (t // coarse_pairs), 4 * (t % coarse_pairs))

    def coarse_finish(t, product):
        for dx in range(2):
            for dy in range(4):
                value = column_of(product, dx, dy, 2)
                x, y = 2 * (t // coarse_pairs) + dx, 4 * (t % coarse_pairs) + dy
                ca[x, y] = leaky(value).astype(BF16)
                total = (
                    sg[2 * x, 2 * y]
                    + sg[2 * x, 2 * y + 1]
                    + sg[2 * x + 1, 2 * y]
                    + sg[2 * x + 1, 2 * y + 1]
                )
                cg[x, y] = (pair_sum(total) * slope(value)).astype(BF16)

    pipelined((cx + 4) // 2 * coarse_pairs, 3, coarse_product, coarse_finish, even, odd)

    @pl.loop(0, (cx + 2) // 2, unroll=True)
    def _(i):
        blocks = (cy + 2) // 2
        window = jnp.concatenate([window_of(cg, 2 * i, 2 * j) for j in range(blocks)], axis=1)
        product = jnp.dot(t3b_ref[...], window, preferred_element_type=F32)
        for dx in range(2):
            for dy in range(2 * blocks):
                pg[2 * i + dx, dy] = column_of(product, dx, dy, 2)

    @pl.loop(0, nx + 2, unroll=3)
    def _(x):
        up = (x + 1) // 2
        for y in range(ny + 2):
            right = (y + 1) // 2
            sk[x, y] = (
                a2[x + 5, y + 5].astype(F32) + ca[up + 1, right + 1].astype(F32)
            ).astype(BF16)
            g2[x, y] = (
                (sg[x + 3, y + 3] + pg[up, right] * 0.125) * slope(p2[x + 5, y + 5])
            ).astype(BF16)

    row, column = (lax.broadcasted_iota(jnp.int32, (CH, CH), axis) for axis in range(2))
    parity = (column == 2 * (row % 32) + row // 32).astype(BF16)

    @pl.loop(0, nx, unroll=True)
    def _(x):
        values = jnp.dot(parity, line(g2, x + 1, 1, ny), preferred_element_type=F32)
        for y in range(ny):
            value = values[:, LANES * y : LANES * (y + 1)]
            g3[x, y] = three_taps(value, 1)

    for x in range(cx):
        values = jnp.dot(parity, line(cg, x + 2, 2, cy), preferred_element_type=F32)
        for y in range(cy):
            c3[x, y] = three_taps(values[:, LANES * y : LANES * (y + 1)], 2)

    fine_pairs = ny // 4

    def back_product(t):
        return product_pair(g2, t2b_ref, 2 * (t // fine_pairs), 4 * (t % fine_pairs))

    def back_finish(t, product):
        for dx in range(2):
            for dy in range(4):
                x, y = 2 * (t // fine_pairs) + dx, 4 * (t % fine_pairs) + dy
                value = column_of(product, dx, dy, 1)
                g1[x, y] = (value * slope(p1[x + 7, y])).astype(BF16)

    pipelined(nx // 2 * fine_pairs, 2, back_product, back_finish, even, odd)

    acc2[...] = jnp.zeros_like(acc2)
    acc4[...] = jnp.zeros_like(acc4)
    acc1[...] = jnp.zeros_like(acc1)

    @pl.loop(0, nx, unroll=4)
    def _(x):
        acc2[...] += contract(
            jnp.concatenate(neighbour_lines(a1, x + 7, 7, ny), axis=0), line(g3, x, 0, ny)
        )
        acc4[...] += contract(
            jnp.concatenate(neighbour_lines(sk, x + 1, 1, ny), axis=0),
            line(f2, x + HALO, HALO, ny),
        )
        acc1[...] += contract(
            jnp.concatenate(neighbour_lines(f1, x + HALO, HALO, ny), axis=0), line(g1, x, 0, ny)
        )

    total3 = 0.5 * sum(
        contract(jnp.concatenate(neighbour_lines(ci, x + 3, 3, cy), axis=0), line(c3, x, 0, cy))
        for x in range(cx)
    )
    total2, total3, total4 = (
        upright(total) for total in (acc2[...], total3, acc4[...])
    )
    for tap in range(27):
        grads_ref[32 * tap : 32 * (tap + 1)] = tap_rows(total2, tap).astype(BF16)
        grads_ref[864 + 32 * tap : 896 + 32 * tap] = tap_rows(total3, tap).astype(BF16)
    for k in range(5):
        grads_ref[1728 + 16 * k : 1744 + 16 * k] = total4[
            :, LANES * k : LANES * (k + 1)
        ].astype(BF16)
    grads_ref[1808:1952] = jnp.concatenate([acc1[...], jnp.zeros_like(acc1)], axis=1).astype(BF16)
    grads_ref[1952:] = jnp.zeros((96, LANES), BF16)


def output_kernel(sk, own_ref, t4_ref, out_ref):
    nx, ny = own_ref.shape[:2]

    @pl.loop(0, nx // 2)
    def _(i):
        blocks = ny // 2
        window = jnp.concatenate([window_of(sk, 2 * i, 2 * j) for j in range(blocks)], axis=1)
        product = jnp.dot(t4_ref[...], window, preferred_element_type=F32)
        for dx in range(2):
            for y in range(ny):
                x = 2 * i + dx
                out_ref[x, y] = column_of(product, dx, y, 1) + own_ref[x, y].astype(F32)


def unpack_kernel(total_ref, two_ref, three_ref, last_ref, first_ref, wide):
    wide[...] = total_ref[:1728].astype(F32)
    for half in range(32):
        lanes = slice(LANES * half, LANES * (half + 1))
        two_ref[:, lanes] = wide[pl.ds(half, 27, stride=32)]
        three_ref[:, lanes] = wide[pl.ds(864 + half, 27, stride=32)]
    for k in range(5):
        last_ref[:, LANES * k : LANES * (k + 1)] = total_ref[
            1728 + 16 * k : 1744 + 16 * k
        ].astype(F32)
    first_ref[...] = total_ref[1808:1952].astype(F32)


def in_vmem(count):
    return [pl.BlockSpec(memory_space=pltpu.VMEM)] * count


def body(field_in, cotangent, kernel_one, kernel_two, kernel_three, kernel_four):
    nx, ny, nz = field_in.shape[1:]
    devices = lax.axis_size("gx") * lax.axis_size("gy")
    scale = 1.0 / math.sqrt(nx * ny * nz * devices)

    blank = jnp.zeros((1, nx, ny, nz), BF16)
    block = jnp.concatenate([field_in, blank, cotangent, blank], axis=0)
    own = jnp.transpose(block, (1, 2, 0, 3))
    block = jnp.concatenate([shifted(own, "gy", 1), own, shifted(own, "gy", -1)], axis=1)
    block, kernel_two, kernel_three = lax.optimization_barrier(
        (block, kernel_two, kernel_three)
    )
    below2, below1 = shifted(block, "gx", 2), shifted(block, "gx", 1)
    above1, above2 = shifted(block, "gx", -1), shifted(block, "gx", -2)
    blocks = (below2, below1, block, above1, above2)

    t2, t2b, t3, t3b = pl.pallas_call(
        weights_kernel,
        out_shape=[jax.ShapeDtypeStruct((6 * CH, 12 * CH), BF16)] * 4,
        in_specs=in_vmem(2),
        out_specs=in_vmem(4),
        cost_estimate=pl.CostEstimate(flops=0, bytes_accessed=30_000_000, transcendentals=0),
    )(kernel_two.reshape(27, CH, CH), kernel_three.reshape(27, CH, CH))
    four = jnp.transpose(kernel_four, (2, 3, 4, 0, 1))
    weights = (
        toeplitz_window(jnp.transpose(kernel_one, (0, 2, 3, 4, 1)), FIELD_ROWS),
        t2,
        t2b,
        t3,
        t3b,
        toeplitz_window(jnp.transpose(swapped(four), (3, 0, 1, 2, 4)), GRADIENT_ROWS),
    )

    wide, tall = nx + 2 * HALO, ny + 2 * HALO
    cx, cy = nx // 2, ny // 2

    def fine(more, kind, rows=CH):
        return pltpu.VMEM((nx + 2 * more, ny + 2 * more, rows, LANES), kind)

    def coarse(more, kind, rows=CH):
        return pltpu.VMEM((cx + 2 * more, cy + 2 * more, rows, LANES), kind)

    skip_sum, grads = pl.pallas_call(
        lambda *refs: step_kernel(scale, nx, ny, *refs),
        out_shape=[
            jax.ShapeDtypeStruct((nx + 2, ny + 2, CH, LANES), BF16),
            jax.ShapeDtypeStruct((2048, LANES), BF16),
        ],
        in_specs=in_vmem(11),
        out_specs=in_vmem(2),
        scratch_shapes=[
            fine(HALO, BF16, 16),
            fine(HALO, BF16, 16),
            fine(7, BF16),
            pltpu.VMEM((nx + 14, ny, CH, LANES), F32),
            fine(6, BF16),
            fine(6, F32),
            fine(4, F32),
            coarse(3, BF16),
            coarse(2, BF16),
            coarse(2, BF16),
            coarse(1, F32),
            fine(1, BF16),
            fine(0, BF16, 3 * CH),
            coarse(0, BF16, 3 * CH),
            fine(0, BF16),
            pltpu.VMEM((9 * CH, 3 * CH), F32),
            pltpu.VMEM((9 * CH, 16), F32),
            pltpu.VMEM((144, CH), F32),
            pltpu.VMEM((6 * CH, 4 * LANES), F32),
            pltpu.VMEM((6 * CH, 4 * LANES), F32),
            pltpu.VMEM((4 * CH, (ny + 14) // 2 * LANES), F32),
            pltpu.VMEM((4 * CH, (ny + 14) // 2 * LANES), F32),
        ],
        compiler_params=pltpu.CompilerParams(vmem_limit_bytes=60 * 1024 * 1024),
    )(*blocks, *weights)

    t4 = toeplitz_rows(jnp.pad(four, ((0, 0), (0, 0), (0, 0), (0, 5), (0, 0))))
    out = pl.pallas_call(
        output_kernel,
        out_shape=jax.ShapeDtypeStruct((nx, ny, 8, LANES), F32),
        in_specs=in_vmem(3),
        out_specs=in_vmem(1)[0],
        cost_estimate=pl.CostEstimate(
            flops=2 * 48 * 12 * CH * nx * ny * LANES // 2, bytes_accessed=2_000_000, transcendentals=0
        ),
    )(skip_sum, own, t4)
    output = jnp.transpose(out[:, :, :3], (2, 0, 1, 3))

    share = lax.all_to_all(grads.reshape(devices, -1, LANES), AXES, 0, 0, tiled=True)
    total = jnp.sum(share.astype(F32), axis=0).astype(BF16)
    total = jnp.broadcast_to(total[None], (devices,) + total.shape)
    total = lax.all_to_all(total, AXES, 0, 0, tiled=True).reshape(2048, LANES)

    grad_two, grad_three, last, first = pl.pallas_call(
        unpack_kernel,
        out_shape=[jax.ShapeDtypeStruct((27, CH * CH), F32)] * 2
        + [
            jax.ShapeDtypeStruct((16, 5 * LANES), F32),
            jax.ShapeDtypeStruct((144, LANES), F32),
        ],
        in_specs=in_vmem(1),
        out_specs=in_vmem(4),
        scratch_shapes=[pltpu.VMEM((1728, LANES), F32)],
    )(total)
    groups = [last[4 * k : 4 * k + 3, : 9 * CH] for k in range(4)]
    taps = [groups[GRADIENT_ROWS.index(2 - e)] for e in range(3)]
    taps = jnp.stack(taps, axis=2).reshape(3, 3, 3, CH, 3)
    grad_four = jnp.transpose(taps, (0, 3, 1, 2, 4))
    first = first[:, :CH].reshape(3, 3, 4, 4, CH)
    taps = jnp.stack([first[:, :, FIELD_ROWS.index(e), :3] for e in range(3)], axis=2)
    grad_one = jnp.transpose(taps, (4, 3, 0, 1, 2))
    return (output, grad_one, grad_two, grad_three, grad_four)


def solution(mesh):
    return jax.shard_map(
        body,
        mesh=mesh,
        in_specs=(P(None, "gx", "gy", None), P(None, "gx", "gy", None), P(), P(), P(), P()),
        out_specs=(P(None, "gx", "gy", None), P(), P(), P(), P()),
        check_vma=False,
    )
```

```python
import math

import jax
import jax.numpy as jnp
from jax import lax
from jax.experimental import pallas as pl
from jax.experimental.pallas import tpu as pltpu
from jax.sharding import PartitionSpec as P

F32 = jnp.float32
BF16 = jnp.bfloat16
AXES = ("gx", "gy")
HALO = 8
CH = 64
LANES = 128
FIELD_ROWS = (0, 2, 1, None)
GRADIENT_ROWS = (0, 2, None, 1)


def shifted(block, axis, steps):
    count = lax.axis_size(axis)
    return lax.ppermute(block, axis, [(i, (i + steps) % count) for i in range(count)])


def toeplitz_rows(taps):
    low = jnp.pad(taps, ((0, 0), (0, 1), (0, 0), (0, 0), (0, 0)))
    high = jnp.pad(taps, ((0, 0), (1, 0), (0, 0), (0, 0), (0, 0)))
    both = jnp.stack([low, high])
    both = jnp.transpose(both, (0, 3, 4, 1, 2, 5))
    return both.reshape(6 * taps.shape[3], 12 * taps.shape[4])


def weights_kernel(two_ref, three_ref, t2_ref, t2b_ref, t3_ref, t3b_ref):
    row, column = (lax.broadcasted_iota(jnp.int32, (CH, CH), axis) for axis in range(2))
    eye = (row == column).astype(BF16)
    zero = jnp.zeros((CH, CH), BF16)
    for source, forward, backward in (
        (two_ref, t2_ref, t2b_ref),
        (three_ref, t3_ref, t3b_ref),
    ):
        for a in range(3):
            for e in range(3):
                taps = [source[9 * a + 3 * b + e] for b in range(3)]
                plain = jnp.concatenate([tap.astype(F32) for tap in taps + [zero]], axis=1)
                turn = contract(eye, jnp.concatenate(taps[::-1] + [zero], axis=0))
                for target, values, at, lane in (
                    (forward, plain, CH * e, 4 * CH * a),
                    (backward, turn, CH * (2 - e), 4 * CH * (2 - a)),
                ):
                    lanes = slice(lane, lane + 4 * CH)
                    target[at : at + CH, lanes] = values.astype(BF16)
                    moved = pltpu.roll(values, CH, 1).astype(BF16)
                    target[at + 3 * CH : at + 4 * CH, lanes] = moved


def toeplitz_window(taps, places):
    taps = jnp.pad(taps, ((0, 0),) * 4 + ((0, 1),))
    zero = jnp.zeros_like(taps[:, :, :, 0])
    taps = jnp.concatenate([zero if e is None else taps[:, :, :, e] for e in places], axis=3)
    rows = [
        jnp.pad(taps, ((0, 0), (dx, 1 - dx), (dy, 1 - dy), (0, 0)))
        for dx in range(2)
        for dy in range(2)
    ]
    return jnp.stack(rows).reshape(4 * taps.shape[0], 256)


def swapped(taps):
    return jnp.swapaxes(jnp.flip(taps, (0, 1, 2)), 3, 4)


def leaky(values):
    return values * (0.55 + 0.45 * jnp.tanh(0.5 * values))


def slope(values):
    sigma = 0.5 + 0.5 * jnp.tanh(0.5 * values)
    return 0.1 + 0.9 * sigma * (1.0 + values * (1.0 - sigma))


def turned(values, steps):
    return pltpu.roll(values, steps % LANES, values.ndim - 1)


def window_of(source, x, y):
    rows = [source[x + r, pl.ds(y, 4)].reshape(4 * CH, LANES) for r in range(4)]
    return jnp.concatenate(
        [jnp.concatenate([rows[a], rows[a + 1]], axis=1) for a in range(3)], axis=0
    )


def product_pair(source, weights, x, y):
    window = jnp.concatenate([window_of(source, x, y), window_of(source, x, y + 2)], axis=1)
    return jnp.dot(weights[...], window, preferred_element_type=F32)


def column_of(product, dx, dy, step):
    out = product.shape[0] // 6
    rows, lane = 3 * out * (dy % 2), LANES * (dx + 2 * (dy // 2))
    first, second, third = (
        product[rows + out * e : rows + out * (e + 1), lane : lane + LANES] for e in range(3)
    )
    return turned(first, step) + second + turned(third, -step)


def pipelined(count, most, product, finish, even, odd):
    odd[...] = jnp.zeros(odd.shape, odd.dtype)
    pairs = count // 2
    many = next(m for m in range(most, 0, -1) if pairs % m == 0)

    @pl.loop(0, pairs // many)
    def _(v):
        for w in range(many):
            t = 2 * (v * many + w)
            even[...] = product(t)
            finish(jnp.maximum(t - 1, 0) if w == 0 else t - 1, odd)
            odd[...] = product(t + 1)
            finish(t, even)

    if count % 2:
        even[...] = product(count - 1)
        finish(count - 2, odd)
        finish(count - 1, even)
    else:
        finish(count - 1, odd)


def window_row(source, weights, x, y, blocks):
    parts = []
    for k in range(blocks):
        rows = [source[x + r, pl.ds(y + 2 * k, 4)].reshape(64, LANES) for r in range(4)]
        parts.append(jnp.concatenate(rows, axis=0))
    return jnp.dot(weights[...], jnp.concatenate(parts, axis=1), preferred_element_type=F32)


def window_column(product, dx, y):
    at, lane = CH * (2 * dx + y % 2), LANES * (y // 2)
    return product[at : at + CH, lane : lane + LANES]


def line(source, x, y, count):
    return jnp.concatenate([source[x, y + k] for k in range(count)], axis=1)


def neighbour_lines(source, x, y, count):
    return [line(source, x + a - 1, y + b - 1, count) for a in range(3) for b in range(3)]


def contract(left, right):
    return lax.dot_general(left, right, (((1,), (1,)), ((), ())), preferred_element_type=F32)


def upright(total):
    count = total.shape[1]
    row, column = (lax.broadcasted_iota(jnp.int32, (count, count), axis) for axis in range(2))
    total = jnp.concatenate([total.astype(BF16), jnp.zeros((CH, count), BF16)], axis=0)
    return contract((row == column).astype(BF16), total)


def three_taps(value, step):
    return jnp.concatenate([turned(value, -step), value, turned(value, step)], axis=0).astype(BF16)


def tap_rows(total, tap):
    place, e = tap // 3, tap % 3
    tile = slice(LANES * (place // 2), LANES * (place // 2 + 1))
    even = total[CH * e : CH * e + 32, tile]
    odd = total[CH * e + 32 : CH * (e + 1), tile]
    left = lax.broadcasted_iota(jnp.int32, even.shape, 1) < CH
    if place % 2 == 0:
        return jnp.where(left, even, turned(odd, CH))
    return jnp.where(left, turned(even, CH), odd)


def pair_sum(values):
    lane = lax.broadcasted_iota(jnp.int32, values.shape, 1)
    return values + jnp.where(lane % 2 == 0, turned(values, -1), turned(values, 1))


def step_kernel(
    scale,
    nx,
    ny,
    below2_ref,
    below1_ref,
    own_ref,
    above1_ref,
    above2_ref,
    t1_ref,
    t2_ref,
    t2b_ref,
    t3_ref,
    t3b_ref,
    t4b_ref,
    sk,
    grads_ref,
    f1,
    f2,
    a1,
    p1,
    a2,
    p2,
    sg,
    ci,
    ca,
    cg,
    pg,
    g2,
    g3,
    c3,
    g1,
    acc2,
    acc4,
    acc1,
    even,
    odd,
    even1,
    odd1,
):
    wide, tall = nx + 2 * HALO, ny + 2 * HALO

    def input_rows(part, first_x):
        @pl.loop(0, nx, unroll=4)
        def _(x):
            cells = part[x].astype(F32)
            first = lax.broadcasted_iota(jnp.int32, cells.shape, 1) < 4
            before, after = turned(cells, 1), turned(cells, -1)
            top = jnp.where(first, before, pltpu.roll(after, 4, 1))
            f1[x + first_x] = jnp.concatenate([top, cells], axis=1).astype(BF16)
            top = jnp.where(first, pltpu.roll(before, 4, 1), after)
            f2[x + first_x] = (jnp.concatenate([top, cells], axis=1) * scale).astype(BF16)

    for k, part in enumerate((below2_ref, below1_ref, own_ref, above1_ref, above2_ref)):
        input_rows(part, k * nx)

    skip_blocks = (ny + 8) // 2

    def skip_product(i):
        return window_row(f2, t4b_ref, 2 * i + 3, 3, skip_blocks)

    def skip_finish(i, product):
        for dx in range(2):
            for y in range(ny + 8):
                sg[2 * i + dx, y] = window_column(product, dx, y)

    lanes = skip_blocks * LANES
    pipelined((nx + 8) // 2, 3, skip_product, skip_finish, even1.at[:, :lanes], odd1.at[:, :lanes])

    def first_product(i):
        return window_row(f1, t1_ref, 2 * i, 0, (ny + 14) // 2)

    def first_finish(i, product):
        for dx in range(2):
            for y in range(ny + 14):
                value = window_column(product, dx, y)
                a1[2 * i + dx, y] = leaky(value).astype(BF16)
                if 0 <= y - 7 < ny:
                    p1[2 * i + dx, y - 7] = value

    pipelined((nx + 14) // 2, 4, first_product, first_finish, even1, odd1)

    pairs = (ny + 12) // 4

    def second_product(t):
        return product_pair(a1, t2_ref, 2 * (t // pairs), 4 * (t % pairs))

    def second_finish(t, product):
        i, j = t // pairs, t % pairs
        for half in range(2):
            total = None
            for dx in range(2):
                for dy in range(2):
                    value = column_of(product, dx, 2 * half + dy, 1)
                    x, y = 2 * i + dx, 4 * j + 2 * half + dy
                    act = leaky(value).astype(BF16)
                    p2[x, y] = value
                    a2[x, y] = act
                    act = act.astype(F32)
                    total = act if total is None else total + act
            ci[i, 2 * j + half] = (pair_sum(total) * 0.125).astype(BF16)

    pipelined((nx + 12) // 2 * pairs, 10, second_product, second_finish, even, odd)

    cx, cy = nx // 2, ny // 2
    coarse_pairs = (cy + 4) // 4

    def coarse_product(t):
        return product_pair(ci, t3_ref, 2 * (t // coarse_pairs), 4 * (t % coarse_pairs))

    def coarse_finish(t, product):
        for dx in range(2):
            for dy in range(4):
                value = column_of(product, dx, dy, 2)
                x, y = 2 * (t // coarse_pairs) + dx, 4 * (t % coarse_pairs) + dy
                ca[x, y] = leaky(value).astype(BF16)
                total = (
                    sg[2 * x, 2 * y]
                    + sg[2 * x, 2 * y + 1]
                    + sg[2 * x + 1, 2 * y]
                    + sg[2 * x + 1, 2 * y + 1]
                )
                cg[x, y] = (pair_sum(total) * slope(value)).astype(BF16)

    pipelined((cx + 4) // 2 * coarse_pairs, 3, coarse_product, coarse_finish, even, odd)

    @pl.loop(0, (cx + 2) // 2, unroll=True)
    def _(i):
        blocks = (cy + 2) // 2
        window = jnp.concatenate([window_of(cg, 2 * i, 2 * j) for j in range(blocks)], axis=1)
        product = jnp.dot(t3b_ref[...], window, preferred_element_type=F32)
        for dx in range(2):
            for dy in range(2 * blocks):
                pg[2 * i + dx, dy] = column_of(product, dx, dy, 2)

    @pl.loop(0, nx + 2, unroll=6)
    def _(x):
        up = (x + 1) // 2
        for y in range(ny + 2):
            right = (y + 1) // 2
            sk[x, y] = (
                a2[x + 5, y + 5].astype(F32) + ca[up + 1, right + 1].astype(F32)
            ).astype(BF16)
            g2[x, y] = (
                (sg[x + 3, y + 3] + pg[up, right] * 0.125) * slope(p2[x + 5, y + 5])
            ).astype(BF16)

    row, column = (lax.broadcasted_iota(jnp.int32, (CH, CH), axis) for axis in range(2))
    parity = (column == 2 * (row % 32) + row // 32).astype(BF16)

    @pl.loop(0, nx, unroll=True)
    def _(x):
        values = jnp.dot(parity, line(g2, x + 1, 1, ny), preferred_element_type=F32)
        for y in range(ny):
            value = values[:, LANES * y : LANES * (y + 1)]
            g3[x, y] = three_taps(value, 1)

    for x in range(cx):
        values = jnp.dot(parity, line(cg, x + 2, 2, cy), preferred_element_type=F32)
        for y in range(cy):
            c3[x, y] = three_taps(values[:, LANES * y : LANES * (y + 1)], 2)

    fine_pairs = ny // 4

    def back_product(t):
        return product_pair(g2, t2b_ref, 2 * (t // fine_pairs), 4 * (t % fine_pairs))

    def back_finish(t, product):
        for dx in range(2):
            for dy in range(4):
                x, y = 2 * (t // fine_pairs) + dx, 4 * (t % fine_pairs) + dy
                value = column_of(product, dx, dy, 1)
                g1[x, y] = (value * slope(p1[x + 7, y])).astype(BF16)

    pipelined(nx // 2 * fine_pairs, 2, back_product, back_finish, even, odd)

    acc2[...] = jnp.zeros_like(acc2)
    acc4[...] = jnp.zeros_like(acc4)
    acc1[...] = jnp.zeros_like(acc1)

    @pl.loop(0, nx, unroll=4)
    def _(x):
        acc2[...] += contract(
            jnp.concatenate(neighbour_lines(a1, x + 7, 7, ny), axis=0), line(g3, x, 0, ny)
        )
        acc4[...] += contract(
            jnp.concatenate(neighbour_lines(sk, x + 1, 1, ny), axis=0),
            line(f2, x + HALO, HALO, ny),
        )
        acc1[...] += contract(
            jnp.concatenate(neighbour_lines(f1, x + HALO, HALO, ny), axis=0), line(g1, x, 0, ny)
        )

    total3 = 0.5 * sum(
        contract(jnp.concatenate(neighbour_lines(ci, x + 3, 3, cy), axis=0), line(c3, x, 0, cy))
        for x in range(cx)
    )
    total2, total3, total4 = (
        upright(total) for total in (acc2[...], total3, acc4[...])
    )
    for tap in range(27):
        grads_ref[32 * tap : 32 * (tap + 1)] = tap_rows(total2, tap).astype(BF16)
        grads_ref[864 + 32 * tap : 896 + 32 * tap] = tap_rows(total3, tap).astype(BF16)
    for k in range(5):
        grads_ref[1728 + 16 * k : 1744 + 16 * k] = total4[
            :, LANES * k : LANES * (k + 1)
        ].astype(BF16)
    grads_ref[1808:1952] = jnp.concatenate([acc1[...], jnp.zeros_like(acc1)], axis=1).astype(BF16)
    grads_ref[1952:] = jnp.zeros((96, LANES), BF16)


def output_kernel(sk, own_ref, t4_ref, out_ref):
    nx, ny = own_ref.shape[:2]

    @pl.loop(0, nx // 2)
    def _(i):
        blocks = ny // 2
        window = jnp.concatenate([window_of(sk, 2 * i, 2 * j) for j in range(blocks)], axis=1)
        product = jnp.dot(t4_ref[...], window, preferred_element_type=F32)
        for dx in range(2):
            for y in range(ny):
                x = 2 * i + dx
                out_ref[x, y] = column_of(product, dx, y, 1) + own_ref[x, y].astype(F32)


def unpack_kernel(total_ref, two_ref, three_ref, last_ref, first_ref, wide):
    wide[...] = total_ref[:1728].astype(F32)
    for half in range(32):
        lanes = slice(LANES * half, LANES * (half + 1))
        two_ref[:, lanes] = wide[pl.ds(half, 27, stride=32)]
        three_ref[:, lanes] = wide[pl.ds(864 + half, 27, stride=32)]
    for k in range(5):
        last_ref[:, LANES * k : LANES * (k + 1)] = total_ref[
            1728 + 16 * k : 1744 + 16 * k
        ].astype(F32)
    first_ref[...] = total_ref[1808:1952].astype(F32)


def in_vmem(count):
    return [pl.BlockSpec(memory_space=pltpu.VMEM)] * count


def body(field_in, cotangent, kernel_one, kernel_two, kernel_three, kernel_four):
    nx, ny, nz = field_in.shape[1:]
    devices = lax.axis_size("gx") * lax.axis_size("gy")
    scale = 1.0 / math.sqrt(nx * ny * nz * devices)

    blank = jnp.zeros((1, nx, ny, nz), BF16)
    block = jnp.concatenate([field_in, blank, cotangent, blank], axis=0)
    own = jnp.transpose(block, (1, 2, 0, 3))
    block = jnp.concatenate([shifted(own, "gy", 1), own, shifted(own, "gy", -1)], axis=1)
    block, kernel_two, kernel_three = lax.optimization_barrier(
        (block, kernel_two, kernel_three)
    )
    below2, below1 = shifted(block, "gx", 2), shifted(block, "gx", 1)
    above1, above2 = shifted(block, "gx", -1), shifted(block, "gx", -2)
    blocks = (below2, below1, block, above1, above2)

    t2, t2b, t3, t3b = pl.pallas_call(
        weights_kernel,
        out_shape=[jax.ShapeDtypeStruct((6 * CH, 12 * CH), BF16)] * 4,
        in_specs=in_vmem(2),
        out_specs=in_vmem(4),
        cost_estimate=pl.CostEstimate(flops=0, bytes_accessed=30_000_000, transcendentals=0),
    )(kernel_two.reshape(27, CH, CH), kernel_three.reshape(27, CH, CH))
    four = jnp.transpose(kernel_four, (2, 3, 4, 0, 1))
    weights = (
        toeplitz_window(jnp.transpose(kernel_one, (0, 2, 3, 4, 1)), FIELD_ROWS),
        t2,
        t2b,
        t3,
        t3b,
        toeplitz_window(jnp.transpose(swapped(four), (3, 0, 1, 2, 4)), GRADIENT_ROWS),
    )

    wide, tall = nx + 2 * HALO, ny + 2 * HALO
    cx, cy = nx // 2, ny // 2

    def fine(more, kind, rows=CH):
        return pltpu.VMEM((nx + 2 * more, ny + 2 * more, rows, LANES), kind)

    def coarse(more, kind, rows=CH):
        return pltpu.VMEM((cx + 2 * more, cy + 2 * more, rows, LANES), kind)

    skip_sum, grads = pl.pallas_call(
        lambda *refs: step_kernel(scale, nx, ny, *refs),
        out_shape=[
            jax.ShapeDtypeStruct((nx + 2, ny + 2, CH, LANES), BF16),
            jax.ShapeDtypeStruct((2048, LANES), BF16),
        ],
        in_specs=in_vmem(11),
        out_specs=in_vmem(2),
        scratch_shapes=[
            fine(HALO, BF16, 16),
            fine(HALO, BF16, 16),
            fine(7, BF16),
            pltpu.VMEM((nx + 14, ny, CH, LANES), F32),
            fine(6, BF16),
            fine(6, F32),
            fine(4, F32),
            coarse(3, BF16),
            coarse(2, BF16),
            coarse(2, BF16),
            coarse(1, F32),
            fine(1, BF16),
            fine(0, BF16, 3 * CH),
            coarse(0, BF16, 3 * CH),
            fine(0, BF16),
            pltpu.VMEM((9 * CH, 3 * CH), F32),
            pltpu.VMEM((9 * CH, 16), F32),
            pltpu.VMEM((144, CH), F32),
            pltpu.VMEM((6 * CH, 4 * LANES), F32),
            pltpu.VMEM((6 * CH, 4 * LANES), F32),
            pltpu.VMEM((4 * CH, (ny + 14) // 2 * LANES), F32),
            pltpu.VMEM((4 * CH, (ny + 14) // 2 * LANES), F32),
        ],
        compiler_params=pltpu.CompilerParams(vmem_limit_bytes=60 * 1024 * 1024),
    )(*blocks, *weights)

    t4 = toeplitz_rows(jnp.pad(four, ((0, 0), (0, 0), (0, 0), (0, 5), (0, 0))))
    out = pl.pallas_call(
        output_kernel,
        out_shape=jax.ShapeDtypeStruct((nx, ny, 8, LANES), F32),
        in_specs=in_vmem(3),
        out_specs=in_vmem(1)[0],
        cost_estimate=pl.CostEstimate(
            flops=2 * 48 * 12 * CH * nx * ny * LANES // 2, bytes_accessed=2_000_000, transcendentals=0
        ),
    )(skip_sum, own, t4)
    output = jnp.transpose(out[:, :, :3], (2, 0, 1, 3))

    share = lax.all_to_all(grads.reshape(devices, -1, LANES), AXES, 0, 0, tiled=True)
    total = jnp.sum(share.astype(F32), axis=0).astype(BF16)
    total = jnp.broadcast_to(total[None], (devices,) + total.shape)
    total = lax.all_to_all(total, AXES, 0, 0, tiled=True).reshape(2048, LANES)

    grad_two, grad_three, last, first = pl.pallas_call(
        unpack_kernel,
        out_shape=[jax.ShapeDtypeStruct((27, CH * CH), F32)] * 2
        + [
            jax.ShapeDtypeStruct((16, 5 * LANES), F32),
            jax.ShapeDtypeStruct((144, LANES), F32),
        ],
        in_specs=in_vmem(1),
        out_specs=in_vmem(4),
        scratch_shapes=[pltpu.VMEM((1728, LANES), F32)],
    )(total)
    groups = [last[4 * k : 4 * k + 3, : 9 * CH] for k in range(4)]
    taps = [groups[GRADIENT_ROWS.index(2 - e)] for e in range(3)]
    taps = jnp.stack(taps, axis=2).reshape(3, 3, 3, CH, 3)
    grad_four = jnp.transpose(taps, (0, 3, 1, 2, 4))
    first = first[:, :CH].reshape(3, 3, 4, 4, CH)
    taps = jnp.stack([first[:, :, FIELD_ROWS.index(e), :3] for e in range(3)], axis=2)
    grad_one = jnp.transpose(taps, (4, 3, 0, 1, 2))
    return (output, grad_one, grad_two, grad_three, grad_four)


def solution(mesh):
    return jax.shard_map(
        body,
        mesh=mesh,
        in_specs=(P(None, "gx", "gy", None), P(None, "gx", "gy", None), P(), P(), P(), P()),
        out_specs=(P(None, "gx", "gy", None), P(), P(), P(), P()),
        check_vma=False,
    )
```
